128 devices in a mesh: dp: 4 (over x), expert: 32 (over y, z, core).
Axes of the slice: x: 4, y: 4, z: 4, core: 2. Of those that a mesh axis runs over, the one named last changes fastest.
Arguments:
- tokens: bfloat16 [16384, 7168], P(('dp', 'expert')), may hold values from -6 to 6
- grad_out: bfloat16 [16384, 7168], P(('dp', 'expert')), may hold values from -1.5 to 1.5
- expert_ids: int32 [16384, 8], P(('dp', 'expert')), may hold values from 0 to 255, as said below
- gate_weights: float32 [16384, 8], P(('dp', 'expert')), may hold values from 0.2 to 1
- w_gate: bfloat16 [7168, 12288], P(None, 'expert'), may hold values from -0.0625 to 0.0625
- w_up: bfloat16 [7168, 12288], P(None, 'expert'), may hold values from -0.0625 to 0.0625
- w_down: bfloat16 [12288, 7168], P('expert'), may hold values from -0.15625 to 0.15625
Outputs:
- grad_tokens: bfloat16 [16384, 7168], P(('dp', 'expert'))
- grad_gate: bfloat16 [7168, 12288], P('dp', 'expert')
- grad_up: bfloat16 [7168, 12288], P('dp', 'expert')
- grad_down: bfloat16 [12288, 7168], P('expert', 'dp')
The draws below stay inside these ranges and needn't reach their ends.
Inputs may be any that keep to these rules, and one draw needn't show every extreme that they name: `expert_ids`: the 8 ids of a token are distinct. Experts 0 to 7 are the experts in flight; no more than 8 tokens of one block of 128 choose any one of them, and in every draw one expert in flight is chosen by exactly 8 tokens of every block.
All inputs are finite; a program needn't handle non-finite values.
Results may differ from the reference program's by a relative error of at most 0.015.
Values may be sent and summed in bfloat16 or wider, within the bound.
A program may use at most 192 MiB of HBM per device.

```python
import jax
import jax.numpy as jnp
from jax import lax

D = 7168
ROUTED = 256
TOPK = 8
HID = 1536
EXPERTS = 8
TOK_DEV = 128
CAP = 8
TOKENS = 16384
N_DP = 4
N_EXPERT = 32


def draw_expert_ids(key, part):
    key = jax.random.fold_in(key, 11)
    blocks = TOKENS // TOK_DEV
    keys = jax.random.split(key, 6)
    fullest = jax.random.randint(keys[0], (), 0, EXPERTS)
    levels = jax.random.randint(keys[1], (EXPERTS,), CAP // 2, CAP + 1)
    counts = jax.random.randint(keys[2], (blocks, EXPERTS), 0, 1 << 20) % levels[None, :] + 1
    counts = jnp.where(jnp.arange(EXPERTS)[None, :] == fullest, CAP, counts)
    scores = jax.random.randint(keys[3], (blocks, EXPERTS, TOK_DEV), 0, 1 << 16)
    scores = scores * TOK_DEV + jnp.arange(TOK_DEV, dtype=jnp.int32)
    ranks = jnp.argsort(jnp.argsort(scores, axis=2), axis=2)
    member = (ranks < counts[..., None]).astype(jnp.int32)
    member = jnp.transpose(member, (0, 2, 1)).reshape(TOKENS, EXPERTS)
    inside = jnp.sum(member, axis=1)
    order = jnp.cumsum(member, axis=1) - 1
    slot_range = jnp.arange(TOPK, dtype=jnp.int32)
    hit = (member[:, :, None] == 1) & (order[:, :, None] == slot_range[None, None, :])
    window_ids = jnp.sum(jnp.where(hit, jnp.arange(EXPERTS, dtype=jnp.int32)[None, :, None], 0), axis=1)
    others = ROUTED - EXPERTS
    filler_scores = jax.random.randint(keys[4], (TOKENS, others), 0, 1 << 16) * others + jnp.arange(others, dtype=jnp.int32)
    filler = jnp.argsort(filler_scores, axis=1)[:, :TOPK].astype(jnp.int32) + EXPERTS
    filler_pos = jnp.clip(slot_range[None, :] - inside[:, None], 0, TOPK - 1)
    filled = jnp.take_along_axis(filler, filler_pos, axis=1)
    ordered_ids = jnp.where(slot_range[None, :] < inside[:, None], window_ids, filled)
    shuffle_scores = jax.random.randint(keys[5], (TOKENS, TOPK), 0, 1 << 16) * TOPK + slot_range[None, :]
    shuffle = jnp.argsort(shuffle_scores, axis=1)
    return jnp.take_along_axis(ordered_ids, shuffle, axis=1).astype(jnp.int32)


def block_levels(stream_key, dims, cuts, low, top_value):
    level = 1.0
    for dim, parts in cuts:
        steps = jax.random.uniform(jax.random.fold_in(jax.random.fold_in(stream_key, 6), dim), (parts,), jnp.float32, low / len(cuts), top_value / len(cuts))
        level = level * jnp.repeat(jnp.exp(steps), dims[dim] // parts).reshape((-1,) + (1,) * (len(dims) - 1 - dim))
    return level


def scatter_about(rng, dims, scale, bound, cuts=(), held_as=jnp.bfloat16):
    array = scale * jax.random.normal(rng, dims, jnp.float32)
    if cuts:
        array = array * block_levels(rng, dims, cuts, -0.22, 0.18)
    return jnp.clip(array, -bound, bound).astype(held_as)


def setup_inputs(seed: int = 0) -> dict:
    key_of = jax.random.split(jax.random.key(seed), 8)
    return {
        "tokens": scatter_about(key_of[0], (TOKENS, D), 1.0, 6.0, ((0, 128),)),
        "grad_out": scatter_about(key_of[1], (TOKENS, D), 0.25, 1.5, ((0, 128),)),
        "expert_ids": draw_expert_ids(jax.random.fold_in(key_of[7], 71), 0),
        "gate_weights": jnp.clip(0.2 + 0.8 * jax.random.uniform(key_of[3], (TOKENS, TOPK), jnp.float32) ** block_levels(key_of[3], (TOKENS, TOPK), ((0, 128),), -0.2, 0.2), 0.2, 1.0),
        "w_gate": scatter_about(key_of[4], (D, EXPERTS * HID), D ** -0.5, 0.0625, ((1, 32),)),
        "w_up": scatter_about(key_of[5], (D, EXPERTS * HID), D ** -0.5, 0.0625, ((1, 32),)),
        "w_down": scatter_about(key_of[6], (EXPERTS * HID, D), HID ** -0.5, 0.15625, ((0, 32),)),
    }


def expert_terms(rows_in, rows_grad, gate_cols, up_cols, down_rows):
    gate_pre = jnp.dot(rows_in, gate_cols, preferred_element_type=jnp.float32)
    up_pre = jnp.dot(rows_in, up_cols, preferred_element_type=jnp.float32)
    sig = jax.nn.sigmoid(gate_pre)
    act = gate_pre * sig
    hidden = (act * up_pre).astype(jnp.bfloat16)
    d_hidden = lax.dot_general(rows_grad, down_rows, (((1,), (1,)), ((), ())), preferred_element_type=jnp.float32)
    d_gate = (d_hidden * up_pre * sig * (1.0 + gate_pre * (1.0 - sig))).astype(jnp.bfloat16)
    d_up = (d_hidden * act).astype(jnp.bfloat16)
    contract_cols = (((1,), (1,)), ((), ()))
    back = lax.dot_general(d_gate, gate_cols, contract_cols, preferred_element_type=jnp.float32)
    back = back + lax.dot_general(d_up, up_cols, contract_cols, preferred_element_type=jnp.float32)
    contract_rows = (((0,), (0,)), ((), ()))
    g_gate = lax.dot_general(rows_in, d_gate, contract_rows, preferred_element_type=jnp.float32)
    g_up = lax.dot_general(rows_in, d_up, contract_rows, preferred_element_type=jnp.float32)
    g_down = lax.dot_general(hidden, rows_grad, contract_rows, preferred_element_type=jnp.float32)
    return back, g_gate, g_up, g_down


def reference(tokens, grad_out, expert_ids, gate_weights, w_gate, w_up, w_down):
    tokens_four = tokens.reshape(N_DP, N_EXPERT, TOK_DEV, D)
    grads_four = grad_out.reshape(N_DP, N_EXPERT, TOK_DEV, D)
    ids_four = expert_ids.reshape(N_DP, N_EXPERT, TOK_DEV, TOPK)
    gates_four = gate_weights.reshape(N_DP, N_EXPERT, TOK_DEV, TOPK)
    slot_range = jnp.arange(CAP, dtype=jnp.int32)

    def one_expert(carry, expert):
        gate_cols = lax.dynamic_slice_in_dim(w_gate, (expert * HID).astype(jnp.int32), HID, 1)
        up_cols = lax.dynamic_slice_in_dim(w_up, (expert * HID).astype(jnp.int32), HID, 1)
        down_rows = lax.dynamic_slice_in_dim(w_down, (expert * HID).astype(jnp.int32), HID, 0)
        sum_gate = jnp.zeros((D, HID), jnp.float32)
        sum_up = jnp.zeros((D, HID), jnp.float32)
        sum_down = jnp.zeros((HID, D), jnp.float32)
        for replica in range(N_DP):
            chosen = ids_four[replica] == expert
            member = jnp.sum(chosen.astype(jnp.int32), axis=2)
            weight = jnp.sum(jnp.where(chosen, gates_four[replica], jnp.float32(0.0)), axis=2)
            position = jnp.cumsum(member, axis=1) - 1
            picker = ((member[..., None] == 1) & (position[..., None] == slot_range)).astype(jnp.float32)
            rows_in = jnp.einsum("jtc,jtd->jcd", picker, tokens_four[replica].astype(jnp.float32), precision=lax.Precision.HIGHEST)
            rows_in = rows_in.astype(jnp.bfloat16).reshape(N_EXPERT * CAP, D)
            rows_raw = jnp.einsum("jtc,jtd->jcd", picker, grads_four[replica].astype(jnp.float32), precision=lax.Precision.HIGHEST)
            slot_gate = jnp.sum(picker * weight[..., None], axis=1)
            rows_grad = (slot_gate[..., None] * rows_raw).astype(jnp.bfloat16).reshape(N_EXPERT * CAP, D)
            back, g_gate, g_up, g_down = expert_terms(rows_in, rows_grad, gate_cols, up_cols, down_rows)
            slot_back = back.astype(jnp.bfloat16).reshape(N_EXPERT, CAP, D)
            returned = jnp.einsum("jtc,jcd->jtd", picker, slot_back.astype(jnp.float32), precision=lax.Precision.HIGHEST)
            carry = carry.at[replica].add(returned)
            sum_gate = sum_gate + g_gate
            sum_up = sum_up + g_up
            sum_down = sum_down + g_down
        return carry, (sum_gate.astype(jnp.bfloat16), sum_up.astype(jnp.bfloat16), sum_down.astype(jnp.bfloat16))

    start = jnp.zeros((N_DP, N_EXPERT, TOK_DEV, D), jnp.float32)
    total, stacked = lax.scan(one_expert, start, jnp.arange(EXPERTS, dtype=jnp.int32))
    grad_tokens = total.reshape(TOKENS, D).astype(jnp.bfloat16)
    grad_gate = jnp.transpose(stacked[0], (1, 0, 2)).reshape(D, EXPERTS * HID)
    grad_up = jnp.transpose(stacked[1], (1, 0, 2)).reshape(D, EXPERTS * HID)
    grad_down = stacked[2].reshape(EXPERTS * HID, D)
    return (grad_tokens, grad_gate, grad_up, grad_down)
```

```python
import jax
import jax.numpy as jnp
from jax import lax
from jax.experimental import pallas as pl
from jax.experimental.pallas import tpu as pltpu
from jax.sharding import PartitionSpec as P

CAP = 8
CHIPS = 16
DP = 4
NCH = 2
KCH = 1024
NB = 256
MESH = pl.DeviceIdType.MESH


def kernel(
    send, pick, wg, wu, wd,
    gt, gg, gu, gd,
    recv, wgu, wdv, xbuf, dall, gu_acc, dh_acc, ret, sib, fin, hid_t, sb,
    w_sem, loc_sem, locx_sem, ds_sem, dr_sem, fs_sem, fr_sem, xs_sem, xr_sem, xfs_sem, xfr_sem,
    gs_sem, gr_sem, ss_sem, sr_sem, rs_sem, rr_sem,
):
    width = wdv.shape[1]
    hid = wdv.shape[0]
    quarter = width // DP
    half = width // 2
    part = half // NCH
    x = lax.axis_index("dp")
    idx = lax.axis_index("expert")
    k = lax.rem(idx, 2)
    chip = idx // 2
    y = chip // 4
    z = lax.rem(chip, 4)
    sibling = (x, chip * 2 + (1 - k))
    mine = k * CHIPS
    other = (1 - k) * CHIPS

    loads = [
        pltpu.make_async_copy(wg, wgu.at[:, pl.ds(0, hid)], w_sem.at[0]),
        pltpu.make_async_copy(wu, wgu.at[:, pl.ds(hid, hid)], w_sem.at[1]),
        pltpu.make_async_copy(wd, wdv, w_sem.at[2]),
    ]

    barrier = pltpu.get_barrier_semaphore()

    def greet(o, carry):
        peer = lax.rem(chip + o, CHIPS)
        pl.semaphore_signal(barrier, inc=1, device_id=(x, peer * 2 + k), device_id_type=MESH)
        return carry

    lax.fori_loop(1, CHIPS, greet, 0)
    for d in range(1, DP):
        pl.semaphore_signal(barrier, inc=1, device_id=(lax.rem(x + d, DP), idx), device_id_type=MESH)
    pl.semaphore_signal(barrier, inc=1, device_id=sibling, device_id_type=MESH)
    pl.semaphore_wait(barrier, CHIPS - 1 + DP - 1 + 1)

    def chip_at(dy, dz, sign):
        return lax.rem(y + sign * dy + 4, 4) * 4 + lax.rem(z + sign * dz + 4, 4)

    def dispatch(dy, dz):
        to = chip_at(dy, dz, 1)
        return pltpu.make_async_remote_copy(
            src_ref=send.at[to // 2],
            dst_ref=recv.at[mine + chip],
            send_sem=ds_sem.at[dy * 4 + dz],
            recv_sem=dr_sem.at[dy * 4 + dz],
            device_id=(x, to * 2 + k),
            device_id_type=MESH,
        )

    own = pltpu.make_async_copy(send.at[chip // 2], recv.at[mine + chip], loc_sem)
    for dy in range(4):
        for dz in range(4):
            if dy == 0 and dz == 0:
                own.start()
            else:
                dispatch(dy, dz).start()
    for load in loads:
        load.start()

    def forward(dy):
        at = pl.ds(mine + lax.rem(y - dy + 4, 4) * 4, 4)
        return pltpu.make_async_remote_copy(
            src_ref=recv.at[at], dst_ref=recv.at[at],
            send_sem=fs_sem.at[dy], recv_sem=fr_sem.at[dy],
            device_id=sibling, device_id_type=MESH,
        )

    def exchange(dy, d):
        at = pl.ds(mine + lax.rem(y - dy + 4, 4) * 4, 4)
        to = lax.rem(x + d, DP)
        columns = pl.ds(pl.multiple_of(to * quarter, 128), quarter)
        return pltpu.make_async_remote_copy(
            src_ref=recv.at[at, :, columns], dst_ref=xbuf.at[x, at],
            send_sem=xs_sem.at[dy * 3 + d - 1], recv_sem=xr_sem.at[dy * 3 + d - 1],
            device_id=(to, idx), device_id_type=MESH,
        )

    def exchange_forward(dy, d):
        at = pl.ds(mine + lax.rem(y - dy + 4, 4) * 4, 4)
        source = lax.rem(x - d + DP, DP)
        return pltpu.make_async_remote_copy(
            src_ref=xbuf.at[source, at], dst_ref=xbuf.at[source, at],
            send_sem=xfs_sem.at[dy * 3 + d - 1], recv_sem=xfr_sem.at[dy * 3 + d - 1],
            device_id=sibling, device_id_type=MESH,
        )

    for dy in range(4):
        for dz in range(4):
            if dy == 0 and dz == 0:
                own.wait()
            else:
                dispatch(dy, dz).wait_recv()
        forward(dy).start()
        for d in range(1, DP):
            exchange(dy, d).start()
        if dy > 0:
            for d in range(1, DP):
                exchange(dy - 1, d).wait_recv()
                exchange_forward(dy - 1, d).start()
    for dy in range(4):
        forward(dy).wait_recv()
    keep = pltpu.make_async_copy(
        recv.at[:, :, pl.ds(pl.multiple_of(x * quarter, 128), quarter)], xbuf.at[x], locx_sem
    )
    keep.start()
    for load in loads:
        load.wait()

    def flat(block, rows):
        return block.astype(jnp.float32).reshape(rows, block.shape[-1]).astype(jnp.bfloat16)

    gu_acc[...] = jnp.zeros_like(gu_acc)
    dh_acc[...] = jnp.zeros_like(dh_acc)

    def contract(i, carry):
        at = pl.ds(pl.multiple_of(i * KCH, KCH), KCH)
        rows_in = flat(recv[:, pl.ds(0, CAP), at], 256)
        rows_grad = flat(recv[:, pl.ds(CAP, CAP), at], 256)
        gu_acc[...] += jnp.dot(rows_in, wgu[at, :], preferred_element_type=jnp.float32)
        dh_acc[...] += lax.dot_general(
            rows_grad, wdv[:, at], (((1,), (1,)), ((), ())), preferred_element_type=jnp.float32
        )
        return carry

    lax.fori_loop(0, width // KCH, contract, 0)

    gate_pre = gu_acc[:, :hid]
    up_pre = gu_acc[:, hid:]
    d_hidden = dh_acc[...]
    sig = jax.nn.sigmoid(gate_pre)
    act = gate_pre * sig
    dall[x, :, pl.ds(0, hid)] = (
        d_hidden * up_pre * sig * (1.0 + gate_pre * (1.0 - sig))
    ).astype(jnp.bfloat16)
    dall[x, :, pl.ds(hid, hid)] = (d_hidden * act).astype(jnp.bfloat16)
    dall[x, :, pl.ds(2 * hid, hid)] = (act * up_pre).astype(jnp.bfloat16)

    def gather(d):
        return pltpu.make_async_remote_copy(
            src_ref=dall.at[x], dst_ref=dall.at[x],
            send_sem=gs_sem.at[d - 1], recv_sem=gr_sem.at[d - 1],
            device_id=(lax.rem(x + d, DP), idx), device_id_type=MESH,
        )

    for d in range(1, DP):
        gather(d).start()

    def to_sibling(q):
        return pltpu.make_async_remote_copy(
            src_ref=ret.at[pl.ds(other, CHIPS), :, pl.ds(q * part, part)],
            dst_ref=sib.at[:, :, pl.ds(q * part, part)],
            send_sem=ss_sem.at[q], recv_sem=sr_sem.at[q],
            device_id=sibling, device_id_type=MESH,
        )

    def give_back(q, dy, dz):
        to = chip_at(dy, dz, 1)
        return pltpu.make_async_remote_copy(
            src_ref=ret.at[mine + to, :, pl.ds(q * part, part)],
            dst_ref=fin.at[chip, :, pl.ds(q * part, part)],
            send_sem=rs_sem.at[q * 16 + dy * 4 + dz], recv_sem=rr_sem.at[q * 16 + dy * 4 + dz],
            device_id=(x, to * 2 + k), device_id_type=MESH,
        )

    def keep_back(q):
        return pltpu.make_async_copy(
            ret.at[mine + chip, :, pl.ds(q * part, part)],
            fin.at[chip, :, pl.ds(q * part, part)],
            rs_sem.at[q * 16],
        )

    for q in range(NCH):
        for h in range(2):
            def back(i, carry, q=q, h=h):
                col = pl.multiple_of(q * part + i * NB, NB)
                out = lax.dot_general(
                    dall[x, :, pl.ds(0, 2 * hid)],
                    wgu[pl.ds(pl.multiple_of(h * half + col, NB), NB), :],
                    (((1,), (1,)), ((), ())),
                    preferred_element_type=jnp.float32,
                )
                ret[:, pl.ds(h * CAP, CAP), pl.ds(col, NB)] = out.reshape(
                    2 * CHIPS, CAP, NB
                ).astype(jnp.bfloat16)
                return carry

            lax.fori_loop(0, part // NB, back, 0)
        to_sibling(q).start()

    for q in range(NCH):
        to_sibling(q).wait_recv()

        def add(i, carry, q=q):
            at = pl.ds(q * part, part)
            ret[mine + i, :, at] = (
                ret[mine + i, :, at].astype(jnp.float32) + sib[i, :, at].astype(jnp.float32)
            ).astype(jnp.bfloat16)
            return carry

        lax.fori_loop(0, CHIPS, add, 0)
        for dy in range(4):
            for dz in range(4):
                if dy == 0 and dz == 0:
                    keep_back(q).start()
                else:
                    give_back(q, dy, dz).start()

    for d in range(1, DP):
        exchange(3, d).wait_recv()
        exchange_forward(3, d).start()
    keep.wait()
    for d in range(1, DP):
        gather(d).wait_recv()
    for dy in range(4):
        for d in range(1, DP):
            exchange_forward(dy, d).wait_recv()
    rows = DP * 2 * CHIPS * CAP
    hid_t[...] = dall[:, :, pl.ds(2 * hid, hid)].reshape(rows, hid).T

    def weights(i, carry):
        at = pl.ds(pl.multiple_of(i * NB, NB), NB)
        rows_in = flat(xbuf[:, :, pl.ds(0, CAP), at], rows)
        rows_grad = flat(xbuf[:, :, pl.ds(CAP, CAP), at], rows)
        out = jnp.dot(
            rows_in.T,
            dall[:, :, pl.ds(0, 2 * hid)].reshape(rows, 2 * hid),
            preferred_element_type=jnp.float32,
        )
        gg[at, :] = out[:, :hid].astype(jnp.bfloat16)
        gu[at, :] = out[:, hid:].astype(jnp.bfloat16)
        gd[:, at] = jnp.dot(hid_t[...], rows_grad, preferred_element_type=jnp.float32).astype(
            jnp.bfloat16
        )
        return carry

    lax.fori_loop(0, quarter // NB, weights, 0)

    for q in range(NCH):
        for dy in range(4):
            for dz in range(4):
                if dy == 0 and dz == 0:
                    keep_back(q).wait()
                else:
                    give_back(q, dy, dz).wait_recv()
    pick_v = pick[...]
    for h in range(2):
        def combine(i, carry, h=h):
            col = pl.multiple_of(i * NB, NB)
            for e in range(CHIPS // 2):
                sb[pl.ds(e * CAP, CAP), :] = (
                    fin[2 * e, pl.ds(h * CAP, CAP), pl.ds(col, NB)].astype(jnp.float32)
                    + fin[2 * e + 1, pl.ds(h * CAP, CAP), pl.ds(col, NB)].astype(jnp.float32)
                )
            gt[:, pl.ds(pl.multiple_of(h * half + col, NB), NB)] = jnp.dot(
                pick_v, sb[...].astype(jnp.bfloat16), preferred_element_type=jnp.float32
            ).astype(jnp.bfloat16)
            return carry

        lax.fori_loop(0, half // NB, combine, 0)

    for dy in range(4):
        forward(dy).wait_send()
        for d in range(1, DP):
            exchange(dy, d).wait_send()
            exchange_forward(dy, d).wait_send()
        for dz in range(4):
            if dy or dz:
                dispatch(dy, dz).wait_send()
                for q in range(NCH):
                    give_back(q, dy, dz).wait_send()
    for d in range(1, DP):
        gather(d).wait_send()
    for q in range(NCH):
        to_sibling(q).wait_send()


def body(tokens, grad_out, expert_ids, gate_weights, w_gate, w_up, w_down):
    experts = CHIPS // 2
    width = tokens.shape[1]
    hid = w_gate.shape[1]
    half = width // 2
    quarter = width // DP
    chosen = expert_ids[None, :, :] == jnp.arange(experts, dtype=jnp.int32)[:, None, None]
    member = jnp.sum(chosen.astype(jnp.int32), axis=2)
    weight = jnp.sum(jnp.where(chosen, gate_weights[None, :, :], jnp.float32(0.0)), axis=2)
    position = jnp.cumsum(member, axis=1) - 1
    slot_mask = (member[..., None] == 1) & (position[..., None] == jnp.arange(CAP, dtype=jnp.int32))
    picker = slot_mask.astype(jnp.bfloat16)
    slot_inputs = jnp.einsum(
        "etc,td->ecd", picker, tokens, preferred_element_type=jnp.float32
    ).astype(jnp.bfloat16)
    raw_grads = jnp.einsum("etc,td->ecd", picker, grad_out, preferred_element_type=jnp.float32)
    slot_gate = jnp.sum(slot_mask.astype(jnp.float32) * weight[..., None], axis=1)
    slot_grads = (slot_gate[..., None] * raw_grads).astype(jnp.bfloat16)
    send = jnp.concatenate([slot_inputs, slot_grads], axis=1)
    pick = jnp.transpose(picker, (1, 0, 2)).reshape(tokens.shape[0], experts * CAP)
    any_spec = pl.BlockSpec(memory_space=pl.ANY)
    vmem = pl.BlockSpec(memory_space=pltpu.VMEM)
    bf16 = jnp.bfloat16
    dma = pltpu.SemaphoreType.DMA
    return pl.pallas_call(
        kernel,
        out_shape=(
            jax.ShapeDtypeStruct(tokens.shape, bf16),
            jax.ShapeDtypeStruct((quarter, hid), bf16),
            jax.ShapeDtypeStruct((quarter, hid), bf16),
            jax.ShapeDtypeStruct((hid, quarter), bf16),
        ),
        in_specs=[any_spec, vmem, any_spec, any_spec, any_spec],
        out_specs=(vmem, vmem, vmem, vmem),
        scratch_shapes=[
            pltpu.VMEM((2 * CHIPS, 2 * CAP, width), bf16),
            pltpu.VMEM((width, 2 * hid), bf16),
            pltpu.VMEM((hid, width), bf16),
            pltpu.VMEM((DP, 2 * CHIPS, 2 * CAP, quarter), bf16),
            pltpu.VMEM((DP, 2 * CHIPS * CAP, 3 * hid), bf16),
            pltpu.VMEM((2 * CHIPS * CAP, 2 * hid), jnp.float32),
            pltpu.VMEM((2 * CHIPS * CAP, hid), jnp.float32),
            pltpu.VMEM((2 * CHIPS, 2 * CAP, half), bf16),
            pltpu.VMEM((CHIPS, 2 * CAP, half), bf16),
            pltpu.VMEM((CHIPS, 2 * CAP, half), bf16),
            pltpu.VMEM((hid, DP * 2 * CHIPS * CAP), bf16),
            pltpu.VMEM((experts * CAP, NB), jnp.float32),
            dma((3,)), dma, dma,
            dma((16,)), dma((16,)),
            dma((4,)), dma((4,)),
            dma((12,)), dma((12,)), dma((12,)), dma((12,)),
            dma((3,)), dma((3,)),
            dma((NCH,)), dma((NCH,)),
            dma((16 * NCH,)), dma((16 * NCH,)),
        ],
        compiler_params=pltpu.CompilerParams(
            collective_id=0, has_side_effects=True, vmem_limit_bytes=60 * 1024 * 1024
        ),
        cost_estimate=pl.CostEstimate(
            flops=8 * 2 * 256 * width * hid, bytes_accessed=26_000_000, transcendentals=256 * hid
        ),
    )(send, pick, w_gate, w_up, w_down)


def solution(mesh):
    in_specs = (
        P(("dp", "expert"), None),
        P(("dp", "expert"), None),
        P(("dp", "expert"), None),
        P(("dp", "expert"), None),
        P(None, "expert"),
        P(None, "expert"),
        P("expert", None),
    )
    out_specs = (P(("dp", "expert"), None), P("dp", "expert"), P("dp", "expert"), P("expert", "dp"))
    return jax.shard_map(body, mesh=mesh, in_specs=in_specs, out_specs=out_specs, check_vma=False)
```

```python
import jax
import jax.numpy as jnp
from jax import lax
from jax.experimental import pallas as pl
from jax.experimental.pallas import tpu as pltpu
from jax.sharding import PartitionSpec as P

CAP = 8
ROW = 2 * CAP
DP = 4
EXPERTS = 8
BLOCKS = 32
DY = (0, 1, 3, 2)
PASSES = 2
PER_PASS = len(DY) // PASSES
KCH = 1024
NB = 512
MESH = pl.DeviceIdType.MESH


def flat(block):
    wide = block.astype(jnp.float32).reshape(block.shape[0] * block.shape[1], block.shape[2])
    return wide.astype(jnp.bfloat16)


def exchange_kernel(
    send, wg, wu, wd,
    xbuf, dall, fin,
    recv, mid, wgu, wdv, dloc, gu_acc, dh_acc, ret, sib, zin, zsum,
    w_sem, own_sem, keep_sem, dk_sem, fk_sem,
    ys_sem, yr_sem, zs_sem, zr_sem, fs_sem, fr_sem, xs_sem, xr_sem, xfs_sem, xfr_sem,
    gs_sem, gr_sem, ss_sem, sr_sem, rs_sem, rr_sem, bs_sem, br_sem,
):
    hid, width = wdv.shape
    quarter = width // DP
    x = lax.axis_index("dp")
    idx = lax.axis_index("expert")
    k = lax.rem(idx, 2)
    chip = idx // 2
    y = chip // 4
    z = lax.rem(chip, 4)
    pair = z // 2
    zs = (2 * pair + (1 - lax.rem(z, 2)), 3 - z, lax.rem(z + 2, 4))

    def device(yy, zz, kk):
        return (x, (yy * 4 + zz) * 2 + kk)

    def remote(src, dst, send_sem, recv_sem, to):
        return pltpu.make_async_remote_copy(
            src_ref=src, dst_ref=dst, send_sem=send_sem, recv_sem=recv_sem,
            device_id=to, device_id_type=MESH,
        )

    ahead = [lax.rem(y + dy, 4) for dy in DY]
    behind = [lax.rem(y - dy + 4, 4) for dy in DY]
    sibling = device(y, z, 1 - k)
    peers = [(lax.rem(x + d, DP), idx) for d in range(1, DP)]
    sources = [lax.rem(x - d + DP, DP) for d in range(1, DP)]

    barrier = pltpu.get_barrier_semaphore()
    near = [device(ahead[g], z, k) for g in (1, 2, 3)] + [device(y, t, k) for t in zs]
    for to in near + peers + [sibling]:
        pl.semaphore_signal(barrier, inc=1, device_id=to, device_id_type=MESH)
    pl.semaphore_wait(barrier, 10)

    def own_block(g, zz):
        return g * 8 + k * 4 + zz

    def along_y(g, far):
        expert = 2 * ahead[g] + (1 - pair if far else pair)
        return remote(
            send.at[expert],
            mid.at[g - 1] if far else recv.at[own_block(g, z)],
            ys_sem.at[g * 2 + far], yr_sem.at[g * 2 + far], device(ahead[g], z, k),
        )

    def along_z(g, t):
        if t == 0:
            src = send.at[2 * y + pair] if g == 0 else recv.at[own_block(g, z)]
        else:
            src = send.at[2 * y + 1 - pair] if g == 0 else mid.at[g - 1]
        return remote(
            src, recv.at[own_block(g, z)],
            zs_sem.at[g * 3 + t], zr_sem.at[g * 3 + t], device(y, zs[t], k),
        )

    def z_arrival(g, t):
        at = recv.at[own_block(g, zs[t])]
        return remote(at, at, zs_sem.at[g * 3 + t], zr_sem.at[g * 3 + t], device(y, zs[t], k))

    own = pltpu.make_async_copy(send.at[2 * y + pair], recv.at[own_block(0, z)], own_sem)
    loads = [
        pltpu.make_async_copy(wg, wgu.at[:, pl.ds(0, hid)], w_sem.at[0]),
        pltpu.make_async_copy(wu, wgu.at[:, pl.ds(hid, hid)], w_sem.at[1]),
        pltpu.make_async_copy(wd, wdv, w_sem.at[2]),
    ]

    def forward(g):
        at = recv.at[pl.ds(own_block(g, 0), 4)]
        return remote(at, at, fs_sem.at[g], fr_sem.at[g], sibling)

    def exchange(g, d):
        to = peers[d][0]
        columns = pl.ds(pl.multiple_of(to * quarter, 128), quarter)
        at = pl.ds(own_block(g, 0), 4)
        return remote(
            recv.at[at, :, columns], xbuf.at[x, at],
            xs_sem.at[g * 3 + d], xr_sem.at[g * 3 + d], peers[d],
        )

    def exchange_forward(g, d):
        at = xbuf.at[sources[d], pl.ds(own_block(g, 0), 4)]
        return remote(at, at, xfs_sem.at[g * 3 + d], xfr_sem.at[g * 3 + d], sibling)

    def keep(p):
        at = pl.ds(p * 8 * PER_PASS, 8 * PER_PASS)
        columns = pl.ds(pl.multiple_of(x * quarter, 128), quarter)
        return pltpu.make_async_copy(recv.at[at, :, columns], xbuf.at[x, at], keep_sem.at[p])

    rows = PER_PASS * 8 * CAP

    def gather(p, d):
        at = pl.ds(p * rows, rows)
        return remote(
            dloc.at[at], dall.at[x, at], gs_sem.at[p * 3 + d], gr_sem.at[p * 3 + d], peers[d]
        )

    def keep_terms(p):
        at = pl.ds(p * rows, rows)
        return pltpu.make_async_copy(dloc.at[at], dall.at[x, at], dk_sem.at[p])

    def relay(g):
        for far in (0, 1):
            along_y(g, far).wait_recv()
        for t in range(3):
            along_z(g, t).start()

    def arrive(g):
        if g == 0:
            own.wait()
        for t in range(3):
            z_arrival(g, t).wait_recv()
        forward(g).start()
        for d in range(3):
            exchange(g, d).start()

    def exchanged(g):
        for d in range(3):
            exchange(g, d).wait_recv()
            exchange_forward(g, d).start()

    def terms(p):
        for g in range(p * PER_PASS, (p + 1) * PER_PASS):
            forward(g).wait_recv()
        keep(p).start()
        blocks = pl.ds(p * 8 * PER_PASS, 8 * PER_PASS)
        gu_acc[...] = jnp.zeros_like(gu_acc)
        dh_acc[...] = jnp.zeros_like(dh_acc)

        def contract(i, carry):
            at = pl.ds(pl.multiple_of(i * KCH, KCH), KCH)
            gu_acc[...] += jnp.dot(
                flat(recv[blocks, pl.ds(0, CAP), at]), wgu[at, :],
                preferred_element_type=jnp.float32,
            )
            dh_acc[...] += lax.dot_general(
                flat(recv[blocks, pl.ds(CAP, CAP), at]), wdv[:, at],
                (((1,), (1,)), ((), ())), preferred_element_type=jnp.float32,
            )
            return carry

        lax.fori_loop(0, width // KCH, contract, 0)
        gate_pre = gu_acc[:, :hid]
        up_pre = gu_acc[:, hid:]
        d_hidden = dh_acc[...]
        sig = jax.nn.sigmoid(gate_pre)
        act = gate_pre * sig
        at = pl.ds(p * rows, rows)
        dloc[at, pl.ds(0, hid)] = (
            d_hidden * up_pre * sig * (1.0 + gate_pre * (1.0 - sig))
        ).astype(jnp.bfloat16)
        dloc[at, pl.ds(hid, hid)] = (d_hidden * act).astype(jnp.bfloat16)
        dloc[at, pl.ds(2 * hid, hid)] = (act * up_pre).astype(jnp.bfloat16)
        for d in range(3):
            gather(p, d).start()
        keep_terms(p).start()

    def to_sibling(g):
        return remote(
            ret.at[pl.ds(g * 8 + (1 - k) * 4, 4)], sib.at[pl.ds(g * 4, 4)],
            ss_sem.at[g], sr_sem.at[g], sibling,
        )

    def back(p):
        def columns(b, carry):
            for h in range(2):
                out = lax.dot_general(
                    dloc[pl.ds(p * rows, rows), pl.ds(0, 2 * hid)],
                    wgu[pl.ds(pl.multiple_of(b * 2 * NB + h * NB, NB), NB), :],
                    (((1,), (1,)), ((), ())),
                    preferred_element_type=jnp.float32,
                )
                ret[
                    pl.ds(p * 8 * PER_PASS, 8 * PER_PASS), pl.ds(h * CAP, CAP),
                    pl.ds(pl.multiple_of(b * NB, NB), NB),
                ] = out.reshape(8 * PER_PASS, CAP, NB).astype(jnp.bfloat16)
            return carry

        lax.fori_loop(0, width // (2 * NB), columns, 0)
        for g in range(p * PER_PASS, (p + 1) * PER_PASS):
            to_sibling(g).start()

    def return_z(g, t):
        return remote(
            ret.at[own_block(g, zs[t])], zin.at[g * 4 + z],
            rs_sem.at[g * 3 + t], rr_sem.at[g * 3 + t], device(y, zs[t], k),
        )

    def return_arrival(g, t):
        at = zin.at[g * 4 + zs[t]]
        return remote(at, at, rs_sem.at[g * 3 + t], rr_sem.at[g * 3 + t], device(y, zs[t], k))

    def plus(a, b):
        return (a.astype(jnp.float32) + b.astype(jnp.float32)).astype(jnp.bfloat16)

    def give_back(p):
        for g in range(p * PER_PASS, (p + 1) * PER_PASS):
            to_sibling(g).wait_recv()

            def add(i, carry, g=g):
                at = own_block(g, i)
                ret[at] = plus(ret[at], sib[g * 4 + i])
                return carry

            lax.fori_loop(0, 4, add, 0)
            for t in range(3):
                return_z(g, t).start()
            zin[g * 4 + z] = ret[own_block(g, z)]

    def return_y(g):
        return remote(
            zsum.at[pl.ds(2 * g, 2)], fin.at[pl.ds(2 * y, 2)],
            bs_sem.at[g], br_sem.at[g], device(behind[g], z, k),
        )

    home = pltpu.make_async_copy(zsum.at[pl.ds(0, 2)], fin.at[pl.ds(2 * y, 2)], fk_sem)

    def relay_back(p):
        for g in range(p * PER_PASS, (p + 1) * PER_PASS):
            for t in range(3):
                return_arrival(g, t).wait_recv()

            def add(i, carry, g=g):
                zsum[2 * g + i] = plus(zin[g * 4 + 2 * i], zin[g * 4 + 2 * i + 1])
                return carry

            lax.fori_loop(0, 2, add, 0)
            if g == 0:
                home.start()
            else:
                return_y(g).start()

    own.start()
    for t in range(3):
        along_z(0, t).start()
    for g in (1, 2):
        for far in (0, 1):
            along_y(g, far).start()
    for load in loads:
        load.start()
    relay(1)
    for far in (0, 1):
        along_y(3, far).start()
    arrive(0)
    relay(2)
    arrive(1)
    relay(3)
    for load in loads:
        load.wait()
    terms(0)
    back(0)
    arrive(2)
    exchanged(0)
    arrive(3)
    exchanged(1)
    give_back(0)
    terms(1)
    relay_back(0)
    back(1)
    exchanged(2)
    give_back(1)
    exchanged(3)
    relay_back(1)

    for g in range(4):
        for d in range(3):
            exchange_forward(g, d).wait_recv()
    for p in range(PASSES):
        keep(p).wait()
        keep_terms(p).wait()
        for d in range(3):
            gather(p, d).wait()
    home.wait()
    for g in range(1, 4):
        return_y(g).wait()
        for far in (0, 1):
            along_y(g, far).wait_send()
    for g in range(4):
        for t in range(3):
            along_z(g, t).wait_send()
            return_z(g, t).wait_send()
        for d in range(3):
            exchange(g, d).wait_send()
            exchange_forward(g, d).wait_send()
        forward(g).wait_send()
        to_sibling(g).wait_send()


def finish_kernel(xbuf, dall, fin, pick, gt, gg, gu, gd, hid_t):
    rows = dall.shape[0] * dall.shape[1]
    hid = dall.shape[2] // 3

    @pl.when(pl.program_id(0) == 0)
    def _():
        hid_t[...] = dall[:, :, 2 * hid:].reshape(rows, hid).T

    rows_in = flat(xbuf[:, pl.ds(0, CAP), :])
    rows_grad = flat(xbuf[:, pl.ds(CAP, CAP), :])
    out = jnp.dot(
        rows_in.T, dall[:, :, : 2 * hid].reshape(rows, 2 * hid), preferred_element_type=jnp.float32
    )
    gg[...] = out[:, :hid].astype(jnp.bfloat16)
    gu[...] = out[:, hid:].astype(jnp.bfloat16)
    gd[...] = jnp.dot(hid_t[...], rows_grad, preferred_element_type=jnp.float32).astype(jnp.bfloat16)
    for h in range(2):
        gt[:, pl.ds(h * NB, NB)] = jnp.dot(
            pick[...], flat(fin[:, pl.ds(h * CAP, CAP), :]), preferred_element_type=jnp.float32
        ).astype(jnp.bfloat16)


def body(tokens, grad_out, expert_ids, gate_weights, w_gate, w_up, w_down):
    width = tokens.shape[1]
    hid = w_gate.shape[1]
    half = width // 2
    quarter = width // DP
    slots = BLOCKS * CAP
    chosen = expert_ids[None, :, :] == jnp.arange(EXPERTS, dtype=jnp.int32)[:, None, None]
    member = jnp.sum(chosen.astype(jnp.int32), axis=2)
    weight = jnp.sum(jnp.where(chosen, gate_weights[None, :, :], jnp.float32(0.0)), axis=2)
    position = jnp.cumsum(member, axis=1) - 1
    slot_mask = (member[..., None] == 1) & (position[..., None] == jnp.arange(CAP, dtype=jnp.int32))
    picker = slot_mask.astype(jnp.bfloat16)
    slot_inputs = jnp.einsum(
        "etc,td->ecd", picker, tokens, preferred_element_type=jnp.float32
    ).astype(jnp.bfloat16)
    raw_grads = jnp.einsum("etc,td->ecd", picker, grad_out, preferred_element_type=jnp.float32)
    slot_gate = jnp.sum(slot_mask.astype(jnp.float32) * weight[..., None], axis=1)
    slot_grads = (slot_gate[..., None] * raw_grads).astype(jnp.bfloat16)
    send = jnp.concatenate([slot_inputs, slot_grads], axis=1)
    pick = jnp.transpose(picker, (1, 0, 2)).reshape(tokens.shape[0], EXPERTS * CAP)
    any_spec = pl.BlockSpec(memory_space=pl.ANY)
    bf16 = jnp.bfloat16
    dma = pltpu.SemaphoreType.DMA
    groups = len(DY)
    xbuf, dall, fin = pl.pallas_call(
        exchange_kernel,
        out_shape=(
            jax.ShapeDtypeStruct((DP, BLOCKS, ROW, quarter), bf16),
            jax.ShapeDtypeStruct((DP, slots, 3 * hid), bf16),
            jax.ShapeDtypeStruct((EXPERTS, ROW, half), bf16),
        ),
        in_specs=[any_spec] * 4,
        out_specs=(any_spec,) * 3,
        scratch_shapes=[
            pltpu.VMEM((BLOCKS, ROW, width), bf16),
            pltpu.VMEM((3, ROW, width), bf16),
            pltpu.VMEM((width, 2 * hid), bf16),
            pltpu.VMEM((hid, width), bf16),
            pltpu.VMEM((slots, 3 * hid), bf16),
            pltpu.VMEM((slots // PASSES, 2 * hid), jnp.float32),
            pltpu.VMEM((slots // PASSES, hid), jnp.float32),
            pltpu.VMEM((BLOCKS, ROW, half), bf16),
            pltpu.VMEM((BLOCKS // 2, ROW, half), bf16),
            pltpu.VMEM((BLOCKS // 2, ROW, half), bf16),
            pltpu.VMEM((EXPERTS, ROW, half), bf16),
            dma((3,)), dma, dma((PASSES,)), dma((PASSES,)), dma,
            dma((8,)), dma((8,)), dma((12,)), dma((12,)),
            dma((groups,)), dma((groups,)),
            dma((12,)), dma((12,)), dma((12,)), dma((12,)),
            dma((3 * PASSES,)), dma((3 * PASSES,)),
            dma((groups,)), dma((groups,)), dma((12,)), dma((12,)), dma((groups,)), dma((groups,)),
        ],
        compiler_params=pltpu.CompilerParams(
            collective_id=0, has_side_effects=True, vmem_limit_bytes=60 * 1024 * 1024
        ),
        cost_estimate=pl.CostEstimate(
            flops=5 * 2 * slots * width * hid, bytes_accessed=26_000_000, transcendentals=slots * hid
        ),
    )(send, w_gate, w_up, w_down)

    steps = half // NB
    columns = quarter // steps
    return pl.pallas_call(
        finish_kernel,
        grid=(steps,),
        out_shape=(
            jax.ShapeDtypeStruct(tokens.shape, bf16),
            jax.ShapeDtypeStruct((quarter, hid), bf16),
            jax.ShapeDtypeStruct((quarter, hid), bf16),
            jax.ShapeDtypeStruct((hid, quarter), bf16),
        ),
        in_specs=[
            pl.BlockSpec((DP * BLOCKS, ROW, columns), lambda i: (0, 0, i)),
            pl.BlockSpec((DP, slots, 3 * hid), lambda i: (0, 0, 0)),
            pl.BlockSpec((EXPERTS, ROW, NB), lambda i: (0, 0, i)),
            pl.BlockSpec((tokens.shape[0], EXPERTS * CAP), lambda i: (0, 0)),
        ],
        out_specs=(
            pl.BlockSpec((tokens.shape[0], 2 * NB), lambda i: (0, i)),
            pl.BlockSpec((columns, hid), lambda i: (i, 0)),
            pl.BlockSpec((columns, hid), lambda i: (i, 0)),
            pl.BlockSpec((hid, columns), lambda i: (0, i)),
        ),
        scratch_shapes=[pltpu.VMEM((hid, DP * slots), bf16)],
        compiler_params=pltpu.CompilerParams(vmem_limit_bytes=60 * 1024 * 1024),
        cost_estimate=pl.CostEstimate(
            flops=3 * 2 * slots * width * hid, bytes_accessed=18_000_000, transcendentals=0
        ),
    )(xbuf.reshape(DP * BLOCKS, ROW, quarter), dall, fin, pick)


def solution(mesh):
    in_specs = (
        P(("dp", "expert"), None),
        P(("dp", "expert"), None),
        P(("dp", "expert"), None),
        P(("dp", "expert"), None),
        P(None, "expert"),
        P(None, "expert"),
        P("expert", None),
    )
    out_specs = (P(("dp", "expert"), None), P("dp", "expert"), P("dp", "expert"), P("expert", "dp"))
    return jax.shard_map(body, mesh=mesh, in_specs=in_specs, out_specs=out_specs, check_vma=False)
```

```python
import jax
import jax.numpy as jnp
from jax import lax
from jax.experimental import pallas as pl
from jax.experimental.pallas import tpu as pltpu
from jax.sharding import PartitionSpec as P

CAP = 8
ROW = 2 * CAP
DP = 4
EXPERTS = 8
BLOCKS = 32
DY = (0, 1, 3, 2)
PASSES = ((0, 1), (2,), (3,))
KCH = 1024
NB = 512
MESH = pl.DeviceIdType.MESH


def flat(block):
    wide = block.astype(jnp.float32).reshape(block.shape[0] * block.shape[1], block.shape[2])
    return wide.astype(jnp.bfloat16)


def exchange_kernel(
    tokens, grad_out, ids, weights, wg, wu, wd,
    xbuf, dall, fin, pick,
    tok, grad, send, recv, mid, wgu, wdv, dloc, ret, sib, zin, zsum,
    t_sem, w_sem, own_sem, keep_sem, dk_sem, fk_sem,
    ys_sem, yr_sem, zs_sem, zr_sem, fs_sem, fr_sem, xs_sem, xr_sem, xfs_sem, xfr_sem,
    gs_sem, gr_sem, ss_sem, sr_sem, rs_sem, rr_sem, bs_sem, br_sem,
):
    hid, width = wdv.shape
    quarter = width // DP
    x = lax.axis_index("dp")
    idx = lax.axis_index("expert")
    k = lax.rem(idx, 2)
    chip = idx // 2
    y = chip // 4
    z = lax.rem(chip, 4)
    pair = z // 2
    zs = (2 * pair + (1 - lax.rem(z, 2)), 3 - z, lax.rem(z + 2, 4))

    def device(yy, zz, kk):
        return (x, (yy * 4 + zz) * 2 + kk)

    def remote(src, dst, send_sem, recv_sem, to):
        return pltpu.make_async_remote_copy(
            src_ref=src, dst_ref=dst, send_sem=send_sem, recv_sem=recv_sem,
            device_id=to, device_id_type=MESH,
        )

    ahead = [lax.rem(y + dy, 4) for dy in DY]
    behind = [lax.rem(y - dy + 4, 4) for dy in DY]
    sibling = device(y, z, 1 - k)
    peers = [(lax.rem(x + d, DP), idx) for d in range(1, DP)]
    sources = [lax.rem(x - d + DP, DP) for d in range(1, DP)]

    barrier = pltpu.get_barrier_semaphore()
    around = [device(ahead[g], z, k) for g in (1, 2, 3)] + [device(y, t, k) for t in zs]
    for to in around + peers + [sibling]:
        pl.semaphore_signal(barrier, inc=1, device_id=to, device_id_type=MESH)

    fetch = [
        pltpu.make_async_copy(tokens, tok, t_sem.at[0]),
        pltpu.make_async_copy(grad_out, grad, t_sem.at[1]),
    ]
    for copy in fetch:
        copy.start()
    count = tok.shape[0]
    topk = ids.shape[0]
    slots = EXPERTS * CAP
    ids_t = ids[...].astype(jnp.float32)
    weights_t = weights[...]
    wanted = lax.broadcasted_iota(jnp.int32, (EXPERTS, topk, count), 0).astype(jnp.float32)
    chosen = ids_t[None] == wanted
    member = jnp.sum(jnp.where(chosen, 1.0, 0.0), axis=1)
    weight = jnp.sum(jnp.where(chosen, weights_t[None], 0.0), axis=1)
    upto = lax.broadcasted_iota(jnp.int32, (count, count), 0) <= lax.broadcasted_iota(
        jnp.int32, (count, count), 1
    )
    position = jnp.dot(
        member.astype(jnp.bfloat16), jnp.where(upto, 1.0, 0.0).astype(jnp.bfloat16),
        preferred_element_type=jnp.float32,
    )
    place = lax.broadcasted_iota(jnp.int32, (EXPERTS, CAP, count), 1).astype(jnp.float32) + 1.0
    held = jnp.where((position[:, None, :] == place) & (member[:, None, :] == 1.0), 1.0, 0.0)
    slot_gate = jnp.sum(held * weight[:, None, :], axis=2, keepdims=True).reshape(slots, 1)
    picker = held.reshape(slots, count).astype(jnp.bfloat16)
    pick[...] = picker
    for copy in fetch:
        copy.wait()

    def fill(i, carry):
        at = pl.ds(pl.multiple_of(i * KCH, KCH), KCH)
        slot_inputs = jnp.dot(picker, tok[:, at], preferred_element_type=jnp.float32)
        raw_grads = jnp.dot(picker, grad[:, at], preferred_element_type=jnp.float32)
        send[:, pl.ds(0, CAP), at] = slot_inputs.reshape(EXPERTS, CAP, KCH).astype(jnp.bfloat16)
        send[:, pl.ds(CAP, CAP), at] = (
            (slot_gate * raw_grads).reshape(EXPERTS, CAP, KCH).astype(jnp.bfloat16)
        )
        return carry

    lax.fori_loop(0, width // KCH, fill, 0)
    pl.semaphore_wait(barrier, 10)

    def own_block(g, zz):
        return g * 8 + k * 4 + zz

    def along_y(g, far):
        expert = 2 * ahead[g] + (1 - pair if far else pair)
        return remote(
            send.at[expert],
            mid.at[g - 1] if far else recv.at[own_block(g, z)],
            ys_sem.at[g * 2 + far], yr_sem.at[g * 2 + far], device(ahead[g], z, k),
        )

    def along_z(g, t):
        if t == 0:
            src = send.at[2 * y + pair] if g == 0 else recv.at[own_block(g, z)]
        else:
            src = send.at[2 * y + 1 - pair] if g == 0 else mid.at[g - 1]
        return remote(
            src, recv.at[own_block(g, z)],
            zs_sem.at[g * 3 + t], zr_sem.at[g * 3 + t], device(y, zs[t], k),
        )

    def z_arrival(g, t):
        at = recv.at[own_block(g, zs[t])]
        return remote(at, at, zs_sem.at[g * 3 + t], zr_sem.at[g * 3 + t], device(y, zs[t], k))

    own = pltpu.make_async_copy(send.at[2 * y + pair], recv.at[own_block(0, z)], own_sem)
    loads = [
        pltpu.make_async_copy(wg, wgu.at[:, pl.ds(0, hid)], w_sem.at[0]),
        pltpu.make_async_copy(wu, wgu.at[:, pl.ds(hid, hid)], w_sem.at[1]),
        pltpu.make_async_copy(wd, wdv, w_sem.at[2]),
    ]

    def forward(g):
        at = recv.at[pl.ds(own_block(g, 0), 4)]
        return remote(at, at, fs_sem.at[g], fr_sem.at[g], sibling)

    def exchange(g, d):
        to = peers[d][0]
        columns = pl.ds(pl.multiple_of(to * quarter, 128), quarter)
        at = pl.ds(own_block(g, 0), 4)
        return remote(
            recv.at[at, :, columns], xbuf.at[x, at],
            xs_sem.at[g * 3 + d], xr_sem.at[g * 3 + d], peers[d],
        )

    def exchange_block(g, d, zz):
        to = peers[d][0]
        columns = pl.ds(pl.multiple_of(to * quarter, 128), quarter)
        at = own_block(g, zz)
        return remote(
            recv.at[at, :, columns], xbuf.at[x, at],
            xs_sem.at[g * 3 + d], xr_sem.at[g * 3 + d], peers[d],
        )

    def exchange_forward(g, d):
        at = xbuf.at[sources[d], pl.ds(own_block(g, 0), 4)]
        return remote(at, at, xfs_sem.at[g * 3 + d], xfr_sem.at[g * 3 + d], sibling)

    def blocks_of(p):
        return pl.ds(PASSES[p][0] * 8, len(PASSES[p]) * 8)

    def rows_of(p):
        return pl.ds(PASSES[p][0] * 8 * CAP, len(PASSES[p]) * 8 * CAP)

    def keep(p):
        at = blocks_of(p)
        columns = pl.ds(pl.multiple_of(x * quarter, 128), quarter)
        return pltpu.make_async_copy(recv.at[at, :, columns], xbuf.at[x, at], keep_sem.at[p])

    def gather(p, d):
        at = rows_of(p)
        return remote(
            dloc.at[at], dall.at[x, at], gs_sem.at[p * 3 + d], gr_sem.at[p * 3 + d], peers[d]
        )

    def keep_terms(p):
        at = rows_of(p)
        return pltpu.make_async_copy(dloc.at[at], dall.at[x, at], dk_sem.at[p])

    def near(g):
        if g == 0:
            own.wait()
        else:
            along_y(g, 0).wait_recv()
        for d in range(3):
            exchange_block(g, d, z).start()

    def arrive(g, t):
        z_arrival(g, t).wait_recv()
        for d in range(3):
            exchange_block(g, d, zs[t]).start()

    def exchanged(g):
        for d in range(3):
            exchange(g, d).wait_recv()
            exchange_forward(g, d).start()

    def terms(p):
        for g in PASSES[p]:
            forward(g).wait_recv()
        keep(p).start()
        blocks = blocks_of(p)
        size = len(PASSES[p]) * 8 * CAP
        both = jnp.zeros((size, 2 * hid), jnp.float32)
        d_hidden = jnp.zeros((size, hid), jnp.float32)
        for i in range(width // KCH):
            at = pl.ds(i * KCH, KCH)
            both += jnp.dot(
                flat(recv[blocks, pl.ds(0, CAP), at]), wgu[at, :],
                preferred_element_type=jnp.float32,
            )
            d_hidden += lax.dot_general(
                flat(recv[blocks, pl.ds(CAP, CAP), at]), wdv[:, at],
                (((1,), (1,)), ((), ())), preferred_element_type=jnp.float32,
            )
        gate_pre = both[:, :hid]
        up_pre = both[:, hid:]
        sig = jax.nn.sigmoid(gate_pre)
        act = gate_pre * sig
        at = rows_of(p)
        dloc[at, pl.ds(0, hid)] = (
            d_hidden * up_pre * sig * (1.0 + gate_pre * (1.0 - sig))
        ).astype(jnp.bfloat16)
        dloc[at, pl.ds(hid, hid)] = (d_hidden * act).astype(jnp.bfloat16)
        dloc[at, pl.ds(2 * hid, hid)] = (act * up_pre).astype(jnp.bfloat16)
        for d in range(3):
            gather(p, d).start()
        keep_terms(p).start()

    def to_sibling(g):
        return remote(
            ret.at[pl.ds(g * 8 + (1 - k) * 4, 4)], sib.at[pl.ds(g * 4, 4)],
            ss_sem.at[g], sr_sem.at[g], sibling,
        )

    def back(p):
        def columns(b, carry):
            for h in range(2):
                out = lax.dot_general(
                    dloc[rows_of(p), pl.ds(0, 2 * hid)],
                    wgu[pl.ds(pl.multiple_of(b * 2 * NB + h * NB, NB), NB), :],
                    (((1,), (1,)), ((), ())),
                    preferred_element_type=jnp.float32,
                )
                ret[
                    blocks_of(p), pl.ds(h * CAP, CAP),
                    pl.ds(pl.multiple_of(b * NB, NB), NB),
                ] = out.reshape(8 * len(PASSES[p]), CAP, NB).astype(jnp.bfloat16)
            return carry

        lax.fori_loop(0, width // (2 * NB), columns, 0)
        for g in PASSES[p]:
            to_sibling(g).start()

    def return_z(g, t):
        return remote(
            ret.at[own_block(g, zs[t])], zin.at[g * 4 + z],
            rs_sem.at[g * 3 + t], rr_sem.at[g * 3 + t], device(y, zs[t], k),
        )

    def return_arrival(g, t):
        at = zin.at[g * 4 + zs[t]]
        return remote(at, at, rs_sem.at[g * 3 + t], rr_sem.at[g * 3 + t], device(y, zs[t], k))

    def plus(a, b):
        return (a.astype(jnp.float32) + b.astype(jnp.float32)).astype(jnp.bfloat16)

    def give_back(p):
        for g in PASSES[p]:
            to_sibling(g).wait_recv()

            def add(i, carry, g=g):
                at = own_block(g, i)
                ret[at] = plus(ret[at], sib[g * 4 + i])
                return carry

            lax.fori_loop(0, 4, add, 0)
            for t in range(3):
                return_z(g, t).start()
            zin[g * 4 + z] = ret[own_block(g, z)]

    def return_y(g):
        return remote(
            zsum.at[pl.ds(2 * g, 2)], fin.at[pl.ds(2 * y, 2)],
            bs_sem.at[g], br_sem.at[g], device(behind[g], z, k),
        )

    home = pltpu.make_async_copy(zsum.at[pl.ds(0, 2)], fin.at[pl.ds(2 * y, 2)], fk_sem)

    def relay_back(p):
        for g in PASSES[p]:
            for t in range(3):
                return_arrival(g, t).wait_recv()

            def add(i, carry, g=g):
                zsum[2 * g + i] = plus(zin[g * 4 + 2 * i], zin[g * 4 + 2 * i + 1])
                return carry

            lax.fori_loop(0, 2, add, 0)
            if g == 0:
                home.start()
            else:
                return_y(g).start()

    own.start()
    for t in range(3):
        along_z(0, t).start()
    for far in (0, 1):
        for g in (1, 2):
            along_y(g, far).start()
    for load in loads:
        load.start()
    near(0)
    near(1)
    along_z(1, 0).start()
    near(2)
    for g in (1, 2):
        along_y(g, 1).wait_recv()
    for far in (0, 1):
        along_y(3, far).start()
    for load in loads:
        load.wait()
    arrive(0, 0)
    along_z(1, 1).start()
    arrive(0, 1)
    along_z(1, 2).start()
    arrive(0, 2)
    along_z(2, 0).start()
    forward(0).start()
    arrive(1, 0)
    along_z(2, 1).start()
    arrive(1, 1)
    along_z(2, 2).start()
    near(3)
    along_y(3, 1).wait_recv()
    arrive(1, 2)
    along_z(3, 0).start()
    forward(1).start()
    terms(0)
    arrive(2, 0)
    along_z(3, 1).start()
    arrive(2, 1)
    along_z(3, 2).start()
    back(0)
    arrive(2, 2)
    forward(2).start()
    exchanged(0)
    terms(1)
    give_back(0)
    back(1)
    exchanged(1)
    for t in range(3):
        arrive(3, t)
    forward(3).start()
    give_back(1)
    terms(2)
    back(2)
    give_back(2)
    relay_back(0)
    exchanged(2)
    relay_back(1)
    exchanged(3)
    relay_back(2)

    for g in range(4):
        for d in range(3):
            exchange_forward(g, d).wait_recv()
    for p in range(len(PASSES)):
        keep(p).wait()
        keep_terms(p).wait()
        for d in range(3):
            gather(p, d).wait()
    home.wait()
    for g in range(1, 4):
        return_y(g).wait()
        for far in (0, 1):
            along_y(g, far).wait_send()
    for g in range(4):
        for t in range(3):
            along_z(g, t).wait_send()
            return_z(g, t).wait_send()
        for d in range(3):
            exchange(g, d).wait_send()
            exchange_forward(g, d).wait_send()
        forward(g).wait_send()
        to_sibling(g).wait_send()


def finish_kernel(xbuf, dall, fin, pick, gt, gg, gu, gd, hid_t):
    rows = dall.shape[0] * dall.shape[1]
    hid = dall.shape[2] // 3

    @pl.when(pl.program_id(0) == 0)
    def _():
        hid_t[...] = dall[:, :, 2 * hid:].reshape(rows, hid).T

    blocks = xbuf.shape[0] * xbuf.shape[1]
    rows_in = flat(xbuf[:, :, pl.ds(0, CAP), :].reshape(blocks, CAP, xbuf.shape[3]))
    rows_grad = flat(xbuf[:, :, pl.ds(CAP, CAP), :].reshape(blocks, CAP, xbuf.shape[3]))
    out = jnp.dot(
        rows_in.T, dall[:, :, : 2 * hid].reshape(rows, 2 * hid), preferred_element_type=jnp.float32
    )
    gg[...] = out[:, :hid].astype(jnp.bfloat16)
    gu[...] = out[:, hid:].astype(jnp.bfloat16)
    gd[...] = jnp.dot(hid_t[...], rows_grad, preferred_element_type=jnp.float32).astype(jnp.bfloat16)
    for h in range(2):
        gt[:, pl.ds(h * NB, NB)] = jnp.dot(
            pick[...].T, flat(fin[:, pl.ds(h * CAP, CAP), :]), preferred_element_type=jnp.float32
        ).astype(jnp.bfloat16)


def body(tokens, grad_out, expert_ids, gate_weights, w_gate, w_up, w_down):
    width = tokens.shape[1]
    hid = w_gate.shape[1]
    half = width // 2
    quarter = width // DP
    slots = BLOCKS * CAP
    any_spec = pl.BlockSpec(memory_space=pl.ANY)
    vmem = pl.BlockSpec(memory_space=pltpu.VMEM)
    bf16 = jnp.bfloat16
    dma = pltpu.SemaphoreType.DMA
    groups = len(DY)
    passes = len(PASSES)
    xbuf, dall, fin, pick = pl.pallas_call(
        exchange_kernel,
        out_shape=(
            pltpu.VMEM((DP, BLOCKS, ROW, quarter), bf16),
            pltpu.VMEM((DP, slots, 3 * hid), bf16),
            pltpu.VMEM((EXPERTS, ROW, half), bf16),
            jax.ShapeDtypeStruct((EXPERTS * CAP, tokens.shape[0]), bf16),
        ),
        in_specs=[any_spec] * 2 + [vmem] * 2 + [any_spec] * 3,
        out_specs=(any_spec,) * 3 + (vmem,),
        scratch_shapes=[
            pltpu.VMEM(tokens.shape, bf16),
            pltpu.VMEM(tokens.shape, bf16),
            pltpu.VMEM((EXPERTS, ROW, width), bf16),
            pltpu.VMEM((BLOCKS, ROW, width), bf16),
            pltpu.VMEM((3, ROW, width), bf16),
            pltpu.VMEM((width, 2 * hid), bf16),
            pltpu.VMEM((hid, width), bf16),
            pltpu.VMEM((slots, 3 * hid), bf16),
            pltpu.VMEM((BLOCKS, ROW, half), bf16),
            pltpu.VMEM((BLOCKS // 2, ROW, half), bf16),
            pltpu.VMEM((BLOCKS // 2, ROW, half), bf16),
            pltpu.VMEM((EXPERTS, ROW, half), bf16),
            dma((2,)), dma((3,)), dma, dma((passes,)), dma((passes,)), dma,
            dma((8,)), dma((8,)), dma((12,)), dma((12,)),
            dma((groups,)), dma((groups,)),
            dma((12,)), dma((12,)), dma((12,)), dma((12,)),
            dma((3 * passes,)), dma((3 * passes,)),
            dma((groups,)), dma((groups,)), dma((12,)), dma((12,)), dma((groups,)), dma((groups,)),
        ],
        compiler_params=pltpu.CompilerParams(
            collective_id=0, has_side_effects=True, vmem_limit_bytes=44 * 1024 * 1024
        ),
        cost_estimate=pl.CostEstimate(
            flops=5 * 2 * slots * width * hid, bytes_accessed=26_000_000, transcendentals=slots * hid
        ),
    )(tokens, grad_out, expert_ids.T, gate_weights.T, w_gate, w_up, w_down)

    steps = half // NB
    columns = quarter // steps
    return pl.pallas_call(
        finish_kernel,
        grid=(steps,),
        out_shape=(
            jax.ShapeDtypeStruct(tokens.shape, bf16),
            jax.ShapeDtypeStruct((quarter, hid), bf16),
            jax.ShapeDtypeStruct((quarter, hid), bf16),
            jax.ShapeDtypeStruct((hid, quarter), bf16),
        ),
        in_specs=[
            pl.BlockSpec((DP, BLOCKS, ROW, columns), lambda i: (0, 0, 0, i)),
            pl.BlockSpec((DP, slots, 3 * hid), lambda i: (0, 0, 0)),
            pl.BlockSpec((EXPERTS, ROW, NB), lambda i: (0, 0, i)),
            pl.BlockSpec((EXPERTS * CAP, tokens.shape[0]), lambda i: (0, 0)),
        ],
        out_specs=(
            pl.BlockSpec((tokens.shape[0], 2 * NB), lambda i: (0, i)),
            pl.BlockSpec((columns, hid), lambda i: (i, 0)),
            pl.BlockSpec((columns, hid), lambda i: (i, 0)),
            pl.BlockSpec((hid, columns), lambda i: (0, i)),
        ),
        scratch_shapes=[pltpu.VMEM((hid, DP * slots), bf16)],
        compiler_params=pltpu.CompilerParams(vmem_limit_bytes=20 * 1024 * 1024),
        cost_estimate=pl.CostEstimate(
            flops=3 * 2 * slots * width * hid, bytes_accessed=18_000_000, transcendentals=0
        ),
    )(xbuf, dall, fin, pick)


def solution(mesh):
    in_specs = (
        P(("dp", "expert"), None),
        P(("dp", "expert"), None),
        P(("dp", "expert"), None),
        P(("dp", "expert"), None),
        P(None, "expert"),
        P(None, "expert"),
        P("expert", None),
    )
    out_specs = (P(("dp", "expert"), None), P("dp", "expert"), P("dp", "expert"), P("expert", "dp"))
    return jax.shard_map(body, mesh=mesh, in_specs=in_specs, out_specs=out_specs, check_vma=False)
```

```python
import jax
import jax.numpy as jnp
from jax import lax
from jax.experimental import pallas as pl
from jax.experimental.pallas import tpu as pltpu
from jax.sharding import PartitionSpec as P

CAP = 8
ROW = 2 * CAP
DP = 4
EXPERTS = 8
BLOCKS = 32
DY = (0, 1, 3, 2)
PASSES = ((0, 1), (2, 3))
KCH = 1024
NB = 512
MESH = pl.DeviceIdType.MESH
RELAYED = (True, False)
PARTS = (((0, 7),), ((0, 4), (4, 3)))


def flat(block):
    wide = block.astype(jnp.float32).reshape(block.shape[0] * block.shape[1], block.shape[2])
    return wide.astype(jnp.bfloat16)


def exchange_kernel(
    tokens, grad_out, ids, weights, wg, wu, wd,
    xbuf, dall, fin, pick,
    tok, grad, send, recv, mid, wgu, wdv, dloc, ret, sib, zin, zsum,
    t_sem, w_sem, own_sem, keep_sem, dk_sem, fk_sem,
    ys_sem, yr_sem, zs_sem, zr_sem, fs_sem, fr_sem, xs_sem, xr_sem, xfs_sem, xfr_sem,
    gs_sem, gr_sem, ss_sem, sr_sem, rs_sem, rr_sem, bs_sem, br_sem,
):
    hid, width = wdv.shape
    quarter = width // DP
    x = lax.axis_index("dp")
    idx = lax.axis_index("expert")
    k = lax.rem(idx, 2)
    chip = idx // 2
    y = chip // 4
    z = lax.rem(chip, 4)
    pair = z // 2
    zs = (2 * pair + (1 - lax.rem(z, 2)), 3 - z, lax.rem(z + 2, 4))

    def device(yy, zz, kk):
        return (x, (yy * 4 + zz) * 2 + kk)

    def remote(src, dst, send_sem, recv_sem, to):
        return pltpu.make_async_remote_copy(
            src_ref=src, dst_ref=dst, send_sem=send_sem, recv_sem=recv_sem,
            device_id=to, device_id_type=MESH,
        )

    ahead = [lax.rem(y + dy, 4) for dy in DY]
    behind = [lax.rem(y - dy + 4, 4) for dy in DY]
    sibling = device(y, z, 1 - k)
    peers = [(lax.rem(x + d, DP), idx) for d in range(1, DP)]
    sources = [lax.rem(x - d + DP, DP) for d in range(1, DP)]

    barrier = pltpu.get_barrier_semaphore()
    around = [device(ahead[g], z, k) for g in (1, 2, 3)] + [device(y, t, k) for t in zs]
    for to in around + peers + [sibling]:
        pl.semaphore_signal(barrier, inc=1, device_id=to, device_id_type=MESH)

    fetch = [
        pltpu.make_async_copy(tokens, tok, t_sem.at[0]),
        pltpu.make_async_copy(grad_out, grad, t_sem.at[1]),
    ]
    for copy in fetch:
        copy.start()
    count = tok.shape[0]
    topk = ids.shape[0]
    slots = EXPERTS * CAP
    ids_t = ids[...].astype(jnp.float32)
    weights_t = weights[...]
    wanted = lax.broadcasted_iota(jnp.int32, (EXPERTS, topk, count), 0).astype(jnp.float32)
    chosen = ids_t[None] == wanted
    member = jnp.sum(jnp.where(chosen, 1.0, 0.0), axis=1)
    weight = jnp.sum(jnp.where(chosen, weights_t[None], 0.0), axis=1)
    upto = lax.broadcasted_iota(jnp.int32, (count, count), 0) <= lax.broadcasted_iota(
        jnp.int32, (count, count), 1
    )
    position = jnp.dot(
        member.astype(jnp.bfloat16), jnp.where(upto, 1.0, 0.0).astype(jnp.bfloat16),
        preferred_element_type=jnp.float32,
    )
    place = lax.broadcasted_iota(jnp.int32, (EXPERTS, CAP, count), 1).astype(jnp.float32) + 1.0
    held = jnp.where((position[:, None, :] == place) & (member[:, None, :] == 1.0), 1.0, 0.0)
    slot_gate = jnp.sum(held * weight[:, None, :], axis=2, keepdims=True).reshape(slots, 1)
    picker = held.reshape(slots, count).astype(jnp.bfloat16)
    pick[...] = picker
    for copy in fetch:
        copy.wait()

    def fill(i, carry):
        at = pl.ds(pl.multiple_of(i * KCH, KCH), KCH)
        slot_inputs = jnp.dot(picker, tok[:, at], preferred_element_type=jnp.float32)
        raw_grads = jnp.dot(picker, grad[:, at], preferred_element_type=jnp.float32)
        send[:, pl.ds(0, CAP), at] = slot_inputs.reshape(EXPERTS, CAP, KCH).astype(jnp.bfloat16)
        send[:, pl.ds(CAP, CAP), at] = (
            (slot_gate * raw_grads).reshape(EXPERTS, CAP, KCH).astype(jnp.bfloat16)
        )
        return carry

    lax.fori_loop(0, width // KCH, fill, 0)
    pl.semaphore_wait(barrier, 10)

    def own_block(g, zz):
        return g * 8 + k * 4 + zz

    def along_y(g, far):
        expert = 2 * ahead[g] + (1 - pair if far else pair)
        return remote(
            send.at[expert],
            mid.at[g - 1] if far else recv.at[own_block(g, z)],
            ys_sem.at[g * 2 + far], yr_sem.at[g * 2 + far], device(ahead[g], z, k),
        )

    def along_z(g, t):
        if t == 0:
            src = send.at[2 * y + pair] if g == 0 else recv.at[own_block(g, z)]
        else:
            src = send.at[2 * y + 1 - pair] if g == 0 else mid.at[g - 1]
        return remote(
            src, recv.at[own_block(g, z)],
            zs_sem.at[g * 3 + t], zr_sem.at[g * 3 + t], device(y, zs[t], k),
        )

    def z_arrival(g, t):
        at = recv.at[own_block(g, zs[t])]
        return remote(at, at, zs_sem.at[g * 3 + t], zr_sem.at[g * 3 + t], device(y, zs[t], k))

    own = pltpu.make_async_copy(send.at[2 * y + pair], recv.at[own_block(0, z)], own_sem)
    loads = [
        pltpu.make_async_copy(wg, wgu.at[:, pl.ds(0, hid)], w_sem.at[0]),
        pltpu.make_async_copy(wu, wgu.at[:, pl.ds(hid, hid)], w_sem.at[1]),
        pltpu.make_async_copy(wd, wdv, w_sem.at[2]),
    ]

    def forward(g):
        at = recv.at[pl.ds(own_block(g, 0), 4)]
        return remote(at, at, fs_sem.at[g], fr_sem.at[g], sibling)

    def exchange(g, d):
        to = peers[d][0]
        columns = pl.ds(pl.multiple_of(to * quarter, 128), quarter)
        at = pl.ds(own_block(g, 0), 4)
        return remote(
            recv.at[at, :, columns], xbuf.at[x, at],
            xs_sem.at[g * 3 + d], xr_sem.at[g * 3 + d], peers[d],
        )

    def exchange_block(g, d, zz):
        to = peers[d][0]
        columns = pl.ds(pl.multiple_of(to * quarter, 128), quarter)
        at = own_block(g, zz)
        return remote(
            recv.at[at, :, columns], xbuf.at[x, at],
            xs_sem.at[g * 3 + d], xr_sem.at[g * 3 + d], peers[d],
        )

    def exchange_forward(g, d):
        at = xbuf.at[sources[d], pl.ds(own_block(g, 0), 4)]
        return remote(at, at, xfs_sem.at[g * 3 + d], xfr_sem.at[g * 3 + d], sibling)

    def blocks_of(p):
        return pl.ds(PASSES[p][0] * 8, len(PASSES[p]) * 8)

    def rows_of(p):
        return pl.ds(PASSES[p][0] * 8 * CAP, len(PASSES[p]) * 8 * CAP)

    def keep(p):
        at = blocks_of(p)
        columns = pl.ds(pl.multiple_of(x * quarter, 128), quarter)
        return pltpu.make_async_copy(recv.at[at, :, columns], xbuf.at[x, at], keep_sem.at[p])

    right, left = peers[0], peers[2]
    before, after = sources[0], sources[2]

    def gather(p, side):
        at = rows_of(p)
        return remote(
            dloc.at[at], dall.at[x, at], gs_sem.at[p * 4 + side], gr_sem.at[p * 4 + side],
            left if side else right,
        )

    def gather_far(p):
        at = rows_of(p)
        return remote(
            dloc.at[at], dall.at[x, at], gs_sem.at[p * 4 + 2], gr_sem.at[p * 4 + 2], peers[1]
        )

    def hand_on(p, side):
        size = len(PASSES[p]) * 4 * CAP
        at = dall.at[after if side else before, pl.ds(PASSES[p][0] * 8 * CAP + side * size, size)]
        return remote(
            at, at, gs_sem.at[p * 4 + 2 + side], gr_sem.at[p * 4 + 2 + side],
            left if side else right,
        )

    def spread(p):
        for side in (0, 1):
            gather(p, side).wait_recv()
            hand_on(p, side).start()

    def keep_terms(p):
        at = rows_of(p)
        return pltpu.make_async_copy(dloc.at[at], dall.at[x, at], dk_sem.at[p])

    def near(g):
        if g == 0:
            own.wait()
        else:
            along_y(g, 0).wait_recv()
        for d in range(3):
            exchange_block(g, d, z).start()

    def arrive(g, t):
        z_arrival(g, t).wait_recv()
        for d in range(3):
            exchange_block(g, d, zs[t]).start()

    def exchanged(g):
        for d in range(3):
            exchange(g, d).wait_recv()
            exchange_forward(g, d).start()

    def terms(p):
        for g in PASSES[p]:
            forward(g).wait_recv()
        keep(p).start()
        blocks = blocks_of(p)
        size = len(PASSES[p]) * 8 * CAP
        both = jnp.zeros((size, 2 * hid), jnp.float32)
        d_hidden = jnp.zeros((size, hid), jnp.float32)
        for i in range(width // KCH):
            at = pl.ds(i * KCH, KCH)
            both += jnp.dot(
                flat(recv[blocks, pl.ds(0, CAP), at]), wgu[at, :],
                preferred_element_type=jnp.float32,
            )
            d_hidden += lax.dot_general(
                flat(recv[blocks, pl.ds(CAP, CAP), at]), wdv[:, at],
                (((1,), (1,)), ((), ())), preferred_element_type=jnp.float32,
            )
        gate_pre = both[:, :hid]
        up_pre = both[:, hid:]
        sig = jax.nn.sigmoid(gate_pre)
        act = gate_pre * sig
        at = rows_of(p)
        dloc[at, pl.ds(0, hid)] = (
            d_hidden * up_pre * sig * (1.0 + gate_pre * (1.0 - sig))
        ).astype(jnp.bfloat16)
        dloc[at, pl.ds(hid, hid)] = (d_hidden * act).astype(jnp.bfloat16)
        dloc[at, pl.ds(2 * hid, hid)] = (act * up_pre).astype(jnp.bfloat16)
        for side in (0, 1):
            gather(p, side).start()
        if not RELAYED[p]:
            gather_far(p).start()
        keep_terms(p).start()

    def part_of(g, part):
        first, size = next(PARTS[p] for p in range(len(PASSES)) if g in PASSES[p])[part]
        return pl.ds(first * NB, size * NB)

    def to_sibling(g, part):
        at = part_of(g, part)
        return remote(
            ret.at[pl.ds(g * 8 + (1 - k) * 4, 4), :, at], sib.at[pl.ds(g * 4, 4), :, at],
            ss_sem.at[g * 2 + part], sr_sem.at[g * 2 + part], sibling,
        )

    def back(p, part):
        first, size = PARTS[p][part]

        def columns(i, carry):
            b = first + i
            for h in range(2):
                out = lax.dot_general(
                    dloc[rows_of(p), pl.ds(0, 2 * hid)],
                    wgu[pl.ds(pl.multiple_of(b * 2 * NB + h * NB, NB), NB), :],
                    (((1,), (1,)), ((), ())),
                    preferred_element_type=jnp.float32,
                )
                ret[
                    blocks_of(p), pl.ds(h * CAP, CAP), pl.ds(pl.multiple_of(b * NB, NB), NB)
                ] = out.reshape(8 * len(PASSES[p]), CAP, NB).astype(jnp.bfloat16)
            return carry

        lax.fori_loop(0, size, columns, 0, unroll=True)
        for g in PASSES[p]:
            to_sibling(g, part).start()

    def return_z(g, t, part):
        at = part_of(g, part)
        return remote(
            ret.at[own_block(g, zs[t]), :, at], zin.at[g * 4 + z, :, at],
            rs_sem.at[(g * 3 + t) * 2 + part], rr_sem.at[(g * 3 + t) * 2 + part],
            device(y, zs[t], k),
        )

    def return_arrival(g, t, part):
        at = zin.at[g * 4 + zs[t], :, part_of(g, part)]
        return remote(
            at, at, rs_sem.at[(g * 3 + t) * 2 + part], rr_sem.at[(g * 3 + t) * 2 + part],
            device(y, zs[t], k),
        )

    def plus(a, b):
        return (a.astype(jnp.float32) + b.astype(jnp.float32)).astype(jnp.bfloat16)

    def give_back(p, part):
        for g in PASSES[p]:
            to_sibling(g, part).wait_recv()
            columns = part_of(g, part)

            def add(i, carry, g=g, columns=columns):
                at = own_block(g, i)
                ret[at, :, columns] = plus(ret[at, :, columns], sib[g * 4 + i, :, columns])
                return carry

            lax.fori_loop(0, 4, add, 0)
            for t in range(3):
                return_z(g, t, part).start()
            zin[g * 4 + z, :, columns] = ret[own_block(g, z), :, columns]

    def return_y(g, part):
        at = part_of(g, part)
        return remote(
            zsum.at[pl.ds(2 * g, 2), :, at], fin.at[pl.ds(2 * y, 2), :, at],
            bs_sem.at[g * 2 + part], br_sem.at[g * 2 + part], device(behind[g], z, k),
        )

    home = pltpu.make_async_copy(zsum.at[pl.ds(0, 2)], fin.at[pl.ds(2 * y, 2)], fk_sem)

    def relay_back(p, part):
        for g in PASSES[p]:
            for t in range(3):
                return_arrival(g, t, part).wait_recv()
            columns = part_of(g, part)

            def add(i, carry, g=g, columns=columns):
                zsum[2 * g + i, :, columns] = plus(
                    zin[g * 4 + 2 * i, :, columns], zin[g * 4 + 2 * i + 1, :, columns]
                )
                return carry

            lax.fori_loop(0, 2, add, 0)
            if g == 0:
                home.start()
            else:
                return_y(g, part).start()

    own.start()
    for t in range(3):
        along_z(0, t).start()
    for far in (0, 1):
        for g in (1, 2):
            along_y(g, far).start()
    for load in loads:
        load.start()
    near(0)
    near(1)
    along_z(1, 0).start()
    near(2)
    for g in (1, 2):
        along_y(g, 1).wait_recv()
    for far in (0, 1):
        along_y(3, far).start()
    for load in loads:
        load.wait()
    arrive(0, 0)
    along_z(1, 1).start()
    arrive(0, 1)
    along_z(1, 2).start()
    arrive(0, 2)
    along_z(2, 0).start()
    forward(0).start()
    arrive(1, 0)
    along_z(2, 1).start()
    arrive(1, 1)
    along_z(2, 2).start()
    near(3)
    along_y(3, 1).wait_recv()
    arrive(1, 2)
    along_z(3, 0).start()
    forward(1).start()
    terms(0)
    arrive(2, 0)
    along_z(3, 1).start()
    arrive(2, 1)
    along_z(3, 2).start()
    back(0, 0)
    arrive(2, 2)
    forward(2).start()
    spread(0)
    give_back(0, 0)
    exchanged(0)
    arrive(3, 0)
    arrive(3, 1)
    arrive(3, 2)
    forward(3).start()
    exchanged(1)
    terms(1)
    back(1, 0)
    relay_back(0, 0)
    give_back(1, 0)
    back(1, 1)
    give_back(1, 1)
    exchanged(2)
    relay_back(1, 0)
    exchanged(3)
    relay_back(1, 1)

    for g in range(4):
        for d in range(3):
            exchange_forward(g, d).wait_recv()
    for p in range(len(PASSES)):
        keep(p).wait()
        keep_terms(p).wait()
        for side in (0, 1):
            gather(p, side).wait_send()
            if RELAYED[p]:
                hand_on(p, side).wait()
            else:
                gather(p, side).wait_recv()
        if not RELAYED[p]:
            gather_far(p).wait()
    home.wait()
    for p in range(len(PASSES)):
        for g in PASSES[p]:
            for part in range(len(PARTS[p])):
                to_sibling(g, part).wait_send()
                for t in range(3):
                    return_z(g, t, part).wait_send()
                if g > 0:
                    return_y(g, part).wait()
    for g in range(4):
        if g > 0:
            for far in (0, 1):
                along_y(g, far).wait_send()
        for t in range(3):
            along_z(g, t).wait_send()
        for d in range(3):
            exchange(g, d).wait_send()
            exchange_forward(g, d).wait_send()
        forward(g).wait_send()


def finish_kernel(xbuf, dall, fin, pick, gt, gg, gu, gd, hid_t):
    rows = dall.shape[0] * dall.shape[1]
    hid = dall.shape[2] // 3

    @pl.when(pl.program_id(0) == 0)
    def _():
        hid_t[...] = dall[:, :, 2 * hid:].reshape(rows, hid).T

    blocks = xbuf.shape[0] * xbuf.shape[1]
    rows_in = flat(xbuf[:, :, pl.ds(0, CAP), :].reshape(blocks, CAP, xbuf.shape[3]))
    rows_grad = flat(xbuf[:, :, pl.ds(CAP, CAP), :].reshape(blocks, CAP, xbuf.shape[3]))
    out = jnp.dot(
        rows_in.T, dall[:, :, : 2 * hid].reshape(rows, 2 * hid), preferred_element_type=jnp.float32
    )
    gg[...] = out[:, :hid].astype(jnp.bfloat16)
    gu[...] = out[:, hid:].astype(jnp.bfloat16)
    gd[...] = jnp.dot(hid_t[...], rows_grad, preferred_element_type=jnp.float32).astype(jnp.bfloat16)
    for h in range(2):
        gt[:, pl.ds(h * NB, NB)] = jnp.dot(
            pick[...].T, flat(fin[:, pl.ds(h * CAP, CAP), :]), preferred_element_type=jnp.float32
        ).astype(jnp.bfloat16)


def body(tokens, grad_out, expert_ids, gate_weights, w_gate, w_up, w_down):
    width = tokens.shape[1]
    hid = w_gate.shape[1]
    half = width // 2
    quarter = width // DP
    slots = BLOCKS * CAP
    any_spec = pl.BlockSpec(memory_space=pl.ANY)
    vmem = pl.BlockSpec(memory_space=pltpu.VMEM)
    bf16 = jnp.bfloat16
    dma = pltpu.SemaphoreType.DMA
    groups = len(DY)
    passes = len(PASSES)
    xbuf, dall, fin, pick = pl.pallas_call(
        exchange_kernel,
        out_shape=(
            pltpu.VMEM((DP, BLOCKS, ROW, quarter), bf16),
            pltpu.VMEM((DP, slots, 3 * hid), bf16),
            pltpu.VMEM((EXPERTS, ROW, half), bf16),
            jax.ShapeDtypeStruct((EXPERTS * CAP, tokens.shape[0]), bf16),
        ),
        in_specs=[any_spec] * 2 + [vmem] * 2 + [any_spec] * 3,
        out_specs=(any_spec,) * 3 + (vmem,),
        scratch_shapes=[
            pltpu.VMEM(tokens.shape, bf16),
            pltpu.VMEM(tokens.shape, bf16),
            pltpu.VMEM((EXPERTS, ROW, width), bf16),
            pltpu.VMEM((BLOCKS, ROW, width), bf16),
            pltpu.VMEM((3, ROW, width), bf16),
            pltpu.VMEM((width, 2 * hid), bf16),
            pltpu.VMEM((hid, width), bf16),
            pltpu.VMEM((slots, 3 * hid), bf16),
            pltpu.VMEM((BLOCKS, ROW, half), bf16),
            pltpu.VMEM((BLOCKS // 2, ROW, half), bf16),
            pltpu.VMEM((BLOCKS // 2, ROW, half), bf16),
            pltpu.VMEM((EXPERTS, ROW, half), bf16),
            dma((2,)), dma((3,)), dma, dma((passes,)), dma((passes,)), dma,
            dma((8,)), dma((8,)), dma((12,)), dma((12,)),
            dma((groups,)), dma((groups,)),
            dma((12,)), dma((12,)), dma((12,)), dma((12,)),
            dma((4 * passes,)), dma((4 * passes,)),
            dma((8,)), dma((8,)), dma((24,)), dma((24,)), dma((8,)), dma((8,)),
        ],
        compiler_params=pltpu.CompilerParams(
            collective_id=0, has_side_effects=True, vmem_limit_bytes=44 * 1024 * 1024
        ),
        cost_estimate=pl.CostEstimate(
            flops=5 * 2 * slots * width * hid, bytes_accessed=26_000_000, transcendentals=slots * hid
        ),
    )(tokens, grad_out, expert_ids.T, gate_weights.T, w_gate, w_up, w_down)

    steps = half // NB
    columns = quarter // steps
    return pl.pallas_call(
        finish_kernel,
        grid=(steps,),
        out_shape=(
            jax.ShapeDtypeStruct(tokens.shape, bf16),
            jax.ShapeDtypeStruct((quarter, hid), bf16),
            jax.ShapeDtypeStruct((quarter, hid), bf16),
            jax.ShapeDtypeStruct((hid, quarter), bf16),
        ),
        in_specs=[
            pl.BlockSpec((DP, BLOCKS, ROW, columns), lambda i: (0, 0, 0, i)),
            pl.BlockSpec((DP, slots, 3 * hid), lambda i: (0, 0, 0)),
            pl.BlockSpec((EXPERTS, ROW, NB), lambda i: (0, 0, i)),
            pl.BlockSpec((EXPERTS * CAP, tokens.shape[0]), lambda i: (0, 0)),
        ],
        out_specs=(
            pl.BlockSpec((tokens.shape[0], 2 * NB), lambda i: (0, i)),
            pl.BlockSpec((columns, hid), lambda i: (i, 0)),
            pl.BlockSpec((columns, hid), lambda i: (i, 0)),
            pl.BlockSpec((hid, columns), lambda i: (0, i)),
        ),
        scratch_shapes=[pltpu.VMEM((hid, DP * slots), bf16)],
        compiler_params=pltpu.CompilerParams(vmem_limit_bytes=20 * 1024 * 1024),
        cost_estimate=pl.CostEstimate(
            flops=3 * 2 * slots * width * hid, bytes_accessed=18_000_000, transcendentals=0
        ),
    )(xbuf, dall, fin, pick)


def solution(mesh):
    in_specs = (
        P(("dp", "expert"), None),
        P(("dp", "expert"), None),
        P(("dp", "expert"), None),
        P(("dp", "expert"), None),
        P(None, "expert"),
        P(None, "expert"),
        P("expert", None),
    )
    out_specs = (P(("dp", "expert"), None), P("dp", "expert"), P("dp", "expert"), P("expert", "dp"))
    return jax.shard_map(body, mesh=mesh, in_specs=in_specs, out_specs=out_specs, check_vma=False)
```

```python
import jax
import jax.numpy as jnp
from jax import lax
from jax.experimental import pallas as pl
from jax.experimental.pallas import tpu as pltpu
from jax.sharding import PartitionSpec as P

CAP = 8
ROW = 2 * CAP
DP = 4
EXPERTS = 8
BLOCKS = 32
DY = (0, 1, 3, 2)
PASSES = ((0, 1), (2, 3))
KCH = 1792
NB = 512
MESH = pl.DeviceIdType.MESH
RELAYED = (True, False)
PARTS = (((0, 7),), ((0, 4), (4, 3)))


def flat(block):
    wide = block.astype(jnp.float32).reshape(block.shape[0] * block.shape[1], block.shape[2])
    return wide.astype(jnp.bfloat16)


def exchange_kernel(
    tokens, grad_out, ids, weights, wg, wu, wd,
    xbuf, dall, fin, pick,
    tok, grad, send, recv, mid, wgu, wdv, dloc, ret, sib, zin, zsum,
    t_sem, w_sem, own_sem, keep_sem, dk_sem, fk_sem,
    ys_sem, yr_sem, zs_sem, zr_sem, fs_sem, fr_sem, xs_sem, xr_sem, xfs_sem, xfr_sem,
    gs_sem, gr_sem, ss_sem, sr_sem, rs_sem, rr_sem, bs_sem, br_sem,
):
    hid, width = wdv.shape
    quarter = width // DP
    x = lax.axis_index("dp")
    idx = lax.axis_index("expert")
    k = lax.rem(idx, 2)
    chip = idx // 2
    y = chip // 4
    z = lax.rem(chip, 4)
    pair = z // 2
    zs = (2 * pair + (1 - lax.rem(z, 2)), 3 - z, lax.rem(z + 2, 4))

    def device(yy, zz, kk):
        return (x, (yy * 4 + zz) * 2 + kk)

    def remote(src, dst, send_sem, recv_sem, to):
        return pltpu.make_async_remote_copy(
            src_ref=src, dst_ref=dst, send_sem=send_sem, recv_sem=recv_sem,
            device_id=to, device_id_type=MESH,
        )

    ahead = [lax.rem(y + dy, 4) for dy in DY]
    behind = [lax.rem(y - dy + 4, 4) for dy in DY]
    sibling = device(y, z, 1 - k)
    peers = [(lax.rem(x + d, DP), idx) for d in range(1, DP)]
    sources = [lax.rem(x - d + DP, DP) for d in range(1, DP)]

    barrier = pltpu.get_barrier_semaphore()
    around = [device(ahead[g], z, k) for g in (1, 2, 3)] + [device(y, t, k) for t in zs]
    for to in around + peers + [sibling]:
        pl.semaphore_signal(barrier, inc=1, device_id=to, device_id_type=MESH)

    fetch = [
        pltpu.make_async_copy(tokens, tok, t_sem.at[0]),
        pltpu.make_async_copy(grad_out, grad, t_sem.at[1]),
    ]
    for copy in fetch:
        copy.start()
    count = tok.shape[0]
    topk = ids.shape[0]
    slots = EXPERTS * CAP
    ids_t = ids[...].astype(jnp.float32)
    weights_t = weights[...]
    wanted = lax.broadcasted_iota(jnp.int32, (EXPERTS, topk, count), 0).astype(jnp.float32)
    chosen = ids_t[None] == wanted
    member = jnp.sum(jnp.where(chosen, 1.0, 0.0), axis=1)
    weight = jnp.sum(jnp.where(chosen, weights_t[None], 0.0), axis=1)
    upto = lax.broadcasted_iota(jnp.int32, (count, count), 0) <= lax.broadcasted_iota(
        jnp.int32, (count, count), 1
    )
    position = jnp.dot(
        member.astype(jnp.bfloat16), jnp.where(upto, 1.0, 0.0).astype(jnp.bfloat16),
        preferred_element_type=jnp.float32,
    )
    place = lax.broadcasted_iota(jnp.int32, (EXPERTS, CAP, count), 1).astype(jnp.float32) + 1.0
    held = jnp.where((position[:, None, :] == place) & (member[:, None, :] == 1.0), 1.0, 0.0)
    slot_gate = jnp.sum(held * weight[:, None, :], axis=2, keepdims=True).reshape(slots, 1)
    picker = held.reshape(slots, count).astype(jnp.bfloat16)
    pick[...] = picker
    for copy in fetch:
        copy.wait()

    def fill(i, carry):
        at = pl.ds(pl.multiple_of(i * KCH, KCH), KCH)
        slot_inputs = jnp.dot(picker, tok[:, at], preferred_element_type=jnp.float32)
        raw_grads = jnp.dot(picker, grad[:, at], preferred_element_type=jnp.float32)
        send[:, pl.ds(0, CAP), at] = slot_inputs.reshape(EXPERTS, CAP, KCH).astype(jnp.bfloat16)
        send[:, pl.ds(CAP, CAP), at] = (
            (slot_gate * raw_grads).reshape(EXPERTS, CAP, KCH).astype(jnp.bfloat16)
        )
        return carry

    lax.fori_loop(0, width // KCH, fill, 0)
    pl.semaphore_wait(barrier, 10)

    def own_block(g, zz):
        return g * 8 + k * 4 + zz

    def along_y(g, far):
        expert = 2 * ahead[g] + (1 - pair if far else pair)
        return remote(
            send.at[expert],
            mid.at[g - 1] if far else recv.at[own_block(g, z)],
            ys_sem.at[g * 2 + far], yr_sem.at[g * 2 + far], device(ahead[g], z, k),
        )

    def along_z(g, t):
        if t == 0:
            src = send.at[2 * y + pair] if g == 0 else recv.at[own_block(g, z)]
        else:
            src = send.at[2 * y + 1 - pair] if g == 0 else mid.at[g - 1]
        return remote(
            src, recv.at[own_block(g, z)],
            zs_sem.at[g * 3 + t], zr_sem.at[g * 3 + t], device(y, zs[t], k),
        )

    def z_arrival(g, t):
        at = recv.at[own_block(g, zs[t])]
        return remote(at, at, zs_sem.at[g * 3 + t], zr_sem.at[g * 3 + t], device(y, zs[t], k))

    own = pltpu.make_async_copy(send.at[2 * y + pair], recv.at[own_block(0, z)], own_sem)
    loads = [
        pltpu.make_async_copy(wg, wgu.at[:, pl.ds(0, hid)], w_sem.at[0]),
        pltpu.make_async_copy(wu, wgu.at[:, pl.ds(hid, hid)], w_sem.at[1]),
        pltpu.make_async_copy(wd, wdv, w_sem.at[2]),
    ]

    def forward(g):
        at = recv.at[pl.ds(own_block(g, 0), 4)]
        return remote(at, at, fs_sem.at[g], fr_sem.at[g], sibling)

    def exchange(g, d):
        to = peers[d][0]
        columns = pl.ds(pl.multiple_of(to * quarter, 128), quarter)
        at = pl.ds(own_block(g, 0), 4)
        return remote(
            recv.at[at, :, columns], xbuf.at[x, at],
            xs_sem.at[g * 3 + d], xr_sem.at[g * 3 + d], peers[d],
        )

    def exchange_block(g, d, zz):
        to = peers[d][0]
        columns = pl.ds(pl.multiple_of(to * quarter, 128), quarter)
        at = own_block(g, zz)
        return remote(
            recv.at[at, :, columns], xbuf.at[x, at],
            xs_sem.at[g * 3 + d], xr_sem.at[g * 3 + d], peers[d],
        )

    def exchange_forward(g, d):
        at = xbuf.at[sources[d], pl.ds(own_block(g, 0), 4)]
        return remote(at, at, xfs_sem.at[g * 3 + d], xfr_sem.at[g * 3 + d], sibling)

    def blocks_of(p):
        return pl.ds(PASSES[p][0] * 8, len(PASSES[p]) * 8)

    def rows_of(p):
        return pl.ds(PASSES[p][0] * 8 * CAP, len(PASSES[p]) * 8 * CAP)

    def keep(p):
        at = blocks_of(p)
        columns = pl.ds(pl.multiple_of(x * quarter, 128), quarter)
        return pltpu.make_async_copy(recv.at[at, :, columns], xbuf.at[x, at], keep_sem.at[p])

    right, left = peers[0], peers[2]
    before, after = sources[0], sources[2]

    def gather(p, side):
        at = rows_of(p)
        return remote(
            dloc.at[at], dall.at[x, at], gs_sem.at[p * 4 + side], gr_sem.at[p * 4 + side],
            left if side else right,
        )

    def gather_far(p):
        at = rows_of(p)
        return remote(
            dloc.at[at], dall.at[x, at], gs_sem.at[p * 4 + 2], gr_sem.at[p * 4 + 2], peers[1]
        )

    def hand_on(p, side):
        size = len(PASSES[p]) * 4 * CAP
        at = dall.at[after if side else before, pl.ds(PASSES[p][0] * 8 * CAP + side * size, size)]
        return remote(
            at, at, gs_sem.at[p * 4 + 2 + side], gr_sem.at[p * 4 + 2 + side],
            left if side else right,
        )

    def spread(p):
        for side in (0, 1):
            gather(p, side).wait_recv()
            hand_on(p, side).start()

    def keep_terms(p):
        at = rows_of(p)
        return pltpu.make_async_copy(dloc.at[at], dall.at[x, at], dk_sem.at[p])

    def near(g):
        if g == 0:
            own.wait()
        else:
            along_y(g, 0).wait_recv()
        for d in range(3):
            exchange_block(g, d, z).start()

    def arrive(g, t):
        z_arrival(g, t).wait_recv()
        for d in range(3):
            exchange_block(g, d, zs[t]).start()

    def exchanged(g):
        for d in range(3):
            exchange(g, d).wait_recv()
            exchange_forward(g, d).start()

    def terms(p):
        for g in PASSES[p]:
            forward(g).wait_recv()
        keep(p).start()
        blocks = blocks_of(p)
        size = len(PASSES[p]) * 8 * CAP
        both = jnp.zeros((size, 2 * hid), jnp.float32)
        d_hidden = jnp.zeros((size, hid), jnp.float32)
        for i in range(width // KCH):
            at = pl.ds(i * KCH, KCH)
            both += jnp.dot(
                flat(recv[blocks, pl.ds(0, CAP), at]), wgu[at, :],
                preferred_element_type=jnp.float32,
            )
            d_hidden += lax.dot_general(
                flat(recv[blocks, pl.ds(CAP, CAP), at]), wdv[:, at],
                (((1,), (1,)), ((), ())), preferred_element_type=jnp.float32,
            )
        gate_pre = both[:, :hid]
        up_pre = both[:, hid:]
        sig = jax.nn.sigmoid(gate_pre)
        act = gate_pre * sig
        at = rows_of(p)
        dloc[at, pl.ds(0, hid)] = (
            d_hidden * up_pre * sig * (1.0 + gate_pre * (1.0 - sig))
        ).astype(jnp.bfloat16)
        dloc[at, pl.ds(hid, hid)] = (d_hidden * act).astype(jnp.bfloat16)
        dloc[at, pl.ds(2 * hid, hid)] = (act * up_pre).astype(jnp.bfloat16)
        for side in (0, 1):
            gather(p, side).start()
        if not RELAYED[p]:
            gather_far(p).start()
        keep_terms(p).start()

    def part_of(g, part):
        first, size = next(PARTS[p] for p in range(len(PASSES)) if g in PASSES[p])[part]
        return pl.ds(first * NB, size * NB)

    def to_sibling(g, part):
        at = part_of(g, part)
        return remote(
            ret.at[pl.ds(g * 8 + (1 - k) * 4, 4), :, at], sib.at[pl.ds(g * 4, 4), :, at],
            ss_sem.at[g * 2 + part], sr_sem.at[g * 2 + part], sibling,
        )

    def back(p, part):
        first, size = PARTS[p][part]

        def columns(i, carry):
            b = first + i
            for h in range(2):
                out = lax.dot_general(
                    dloc[rows_of(p), pl.ds(0, 2 * hid)],
                    wgu[pl.ds(pl.multiple_of(b * 2 * NB + h * NB, NB), NB), :],
                    (((1,), (1,)), ((), ())),
                    preferred_element_type=jnp.float32,
                )
                ret[
                    blocks_of(p), pl.ds(h * CAP, CAP), pl.ds(pl.multiple_of(b * NB, NB), NB)
                ] = out.reshape(8 * len(PASSES[p]), CAP, NB).astype(jnp.bfloat16)
            return carry

        lax.fori_loop(0, size, columns, 0, unroll=True)
        for g in PASSES[p]:
            to_sibling(g, part).start()

    def return_z(g, t, part):
        at = part_of(g, part)
        return remote(
            ret.at[own_block(g, zs[t]), :, at], zin.at[g * 4 + z, :, at],
            rs_sem.at[(g * 3 + t) * 2 + part], rr_sem.at[(g * 3 + t) * 2 + part],
            device(y, zs[t], k),
        )

    def return_arrival(g, t, part):
        at = zin.at[g * 4 + zs[t], :, part_of(g, part)]
        return remote(
            at, at, rs_sem.at[(g * 3 + t) * 2 + part], rr_sem.at[(g * 3 + t) * 2 + part],
            device(y, zs[t], k),
        )

    def plus(a, b):
        return (a.astype(jnp.float32) + b.astype(jnp.float32)).astype(jnp.bfloat16)

    def give_back(p, part):
        for g in PASSES[p]:
            to_sibling(g, part).wait_recv()
            columns = part_of(g, part)

            def add(i, carry, g=g, columns=columns):
                at = own_block(g, i)
                ret[at, :, columns] = plus(ret[at, :, columns], sib[g * 4 + i, :, columns])
                return carry

            lax.fori_loop(0, 4, add, 0)
            for t in range(3):
                return_z(g, t, part).start()
            zin[g * 4 + z, :, columns] = ret[own_block(g, z), :, columns]

    def return_y(g, part):
        at = part_of(g, part)
        return remote(
            zsum.at[pl.ds(2 * g, 2), :, at], fin.at[pl.ds(2 * y, 2), :, at],
            bs_sem.at[g * 2 + part], br_sem.at[g * 2 + part], device(behind[g], z, k),
        )

    home = pltpu.make_async_copy(zsum.at[pl.ds(0, 2)], fin.at[pl.ds(2 * y, 2)], fk_sem)

    def relay_back(p, part):
        for g in PASSES[p]:
            for t in range(3):
                return_arrival(g, t, part).wait_recv()
            columns = part_of(g, part)

            def add(i, carry, g=g, columns=columns):
                zsum[2 * g + i, :, columns] = plus(
                    zin[g * 4 + 2 * i, :, columns], zin[g * 4 + 2 * i + 1, :, columns]
                )
                return carry

            lax.fori_loop(0, 2, add, 0)
            if g == 0:
                home.start()
            else:
                return_y(g, part).start()

    own.start()
    for t in range(3):
        along_z(0, t).start()
    for far in (0, 1):
        for g in (1, 2):
            along_y(g, far).start()
    for load in loads:
        load.start()
    near(0)
    near(1)
    along_z(1, 0).start()
    near(2)
    for g in (1, 2):
        along_y(g, 1).wait_recv()
    for far in (0, 1):
        along_y(3, far).start()
    for load in loads:
        load.wait()
    arrive(0, 0)
    along_z(1, 1).start()
    arrive(0, 1)
    along_z(1, 2).start()
    arrive(0, 2)
    along_z(2, 0).start()
    forward(0).start()
    arrive(1, 0)
    along_z(2, 1).start()
    arrive(1, 1)
    along_z(2, 2).start()
    near(3)
    along_y(3, 1).wait_recv()
    arrive(1, 2)
    along_z(3, 0).start()
    forward(1).start()
    terms(0)
    arrive(2, 0)
    along_z(3, 1).start()
    arrive(2, 1)
    along_z(3, 2).start()
    back(0, 0)
    arrive(2, 2)
    forward(2).start()
    spread(0)
    give_back(0, 0)
    exchanged(0)
    arrive(3, 0)
    arrive(3, 1)
    arrive(3, 2)
    forward(3).start()
    terms(1)
    exchanged(1)
    back(1, 0)
    give_back(1, 0)
    relay_back(0, 0)
    back(1, 1)
    give_back(1, 1)
    exchanged(2)
    relay_back(1, 0)
    exchanged(3)
    relay_back(1, 1)

    for g in range(4):
        for d in range(3):
            exchange_forward(g, d).wait_recv()
    for p in range(len(PASSES)):
        keep(p).wait()
        keep_terms(p).wait()
        for side in (0, 1):
            gather(p, side).wait_send()
            if RELAYED[p]:
                hand_on(p, side).wait()
            else:
                gather(p, side).wait_recv()
        if not RELAYED[p]:
            gather_far(p).wait()
    home.wait()
    for p in range(len(PASSES)):
        for g in PASSES[p]:
            for part in range(len(PARTS[p])):
                to_sibling(g, part).wait_send()
                for t in range(3):
                    return_z(g, t, part).wait_send()
                if g > 0:
                    return_y(g, part).wait()
    for g in range(4):
        if g > 0:
            for far in (0, 1):
                along_y(g, far).wait_send()
        for t in range(3):
            along_z(g, t).wait_send()
        for d in range(3):
            exchange(g, d).wait_send()
            exchange_forward(g, d).wait_send()
        forward(g).wait_send()


def finish_kernel(xbuf, dall, fin, pick, gt, gg, gu, gd, hid_t):
    rows = dall.shape[0] * dall.shape[1]
    hid = dall.shape[2] // 3

    @pl.when(pl.program_id(0) == 0)
    def _():
        hid_t[...] = dall[:, :, 2 * hid:].reshape(rows, hid).T

    blocks = xbuf.shape[0] * xbuf.shape[1]
    rows_in = flat(xbuf[:, :, pl.ds(0, CAP), :].reshape(blocks, CAP, xbuf.shape[3]))
    rows_grad = flat(xbuf[:, :, pl.ds(CAP, CAP), :].reshape(blocks, CAP, xbuf.shape[3]))
    out = jnp.dot(
        rows_in.T, dall[:, :, : 2 * hid].reshape(rows, 2 * hid), preferred_element_type=jnp.float32
    )
    gg[...] = out[:, :hid].astype(jnp.bfloat16)
    gu[...] = out[:, hid:].astype(jnp.bfloat16)
    gd[...] = jnp.dot(hid_t[...], rows_grad, preferred_element_type=jnp.float32).astype(jnp.bfloat16)
    for h in range(2):
        gt[:, pl.ds(h * NB, NB)] = jnp.dot(
            pick[...].T, flat(fin[:, pl.ds(h * CAP, CAP), :]), preferred_element_type=jnp.float32
        ).astype(jnp.bfloat16)


def body(tokens, grad_out, expert_ids, gate_weights, w_gate, w_up, w_down):
    width = tokens.shape[1]
    hid = w_gate.shape[1]
    half = width // 2
    quarter = width // DP
    slots = BLOCKS * CAP
    any_spec = pl.BlockSpec(memory_space=pl.ANY)
    vmem = pl.BlockSpec(memory_space=pltpu.VMEM)
    bf16 = jnp.bfloat16
    dma = pltpu.SemaphoreType.DMA
    groups = len(DY)
    passes = len(PASSES)
    xbuf, dall, fin, pick = pl.pallas_call(
        exchange_kernel,
        out_shape=(
            pltpu.VMEM((DP, BLOCKS, ROW, quarter), bf16),
            pltpu.VMEM((DP, slots, 3 * hid), bf16),
            pltpu.VMEM((EXPERTS, ROW, half), bf16),
            jax.ShapeDtypeStruct((EXPERTS * CAP, tokens.shape[0]), bf16),
        ),
        in_specs=[any_spec] * 2 + [vmem] * 2 + [any_spec] * 3,
        out_specs=(any_spec,) * 3 + (vmem,),
        scratch_shapes=[
            pltpu.VMEM(tokens.shape, bf16),
            pltpu.VMEM(tokens.shape, bf16),
            pltpu.VMEM((EXPERTS, ROW, width), bf16),
            pltpu.VMEM((BLOCKS, ROW, width), bf16),
            pltpu.VMEM((3, ROW, width), bf16),
            pltpu.VMEM((width, 2 * hid), bf16),
            pltpu.VMEM((hid, width), bf16),
            pltpu.VMEM((slots, 3 * hid), bf16),
            pltpu.VMEM((BLOCKS, ROW, half), bf16),
            pltpu.VMEM((BLOCKS // 2, ROW, half), bf16),
            pltpu.VMEM((BLOCKS // 2, ROW, half), bf16),
            pltpu.VMEM((EXPERTS, ROW, half), bf16),
            dma((2,)), dma((3,)), dma, dma((passes,)), dma((passes,)), dma,
            dma((8,)), dma((8,)), dma((12,)), dma((12,)),
            dma((groups,)), dma((groups,)),
            dma((12,)), dma((12,)), dma((12,)), dma((12,)),
            dma((4 * passes,)), dma((4 * passes,)),
            dma((8,)), dma((8,)), dma((24,)), dma((24,)), dma((8,)), dma((8,)),
        ],
        compiler_params=pltpu.CompilerParams(
            collective_id=0, has_side_effects=True, vmem_limit_bytes=44 * 1024 * 1024
        ),
        cost_estimate=pl.CostEstimate(
            flops=5 * 2 * slots * width * hid, bytes_accessed=26_000_000, transcendentals=slots * hid
        ),
    )(tokens, grad_out, expert_ids.T, gate_weights.T, w_gate, w_up, w_down)

    steps = half // NB
    columns = quarter // steps
    return pl.pallas_call(
        finish_kernel,
        grid=(steps,),
        out_shape=(
            jax.ShapeDtypeStruct(tokens.shape, bf16),
            jax.ShapeDtypeStruct((quarter, hid), bf16),
            jax.ShapeDtypeStruct((quarter, hid), bf16),
            jax.ShapeDtypeStruct((hid, quarter), bf16),
        ),
        in_specs=[
            pl.BlockSpec((DP, BLOCKS, ROW, columns), lambda i: (0, 0, 0, i)),
            pl.BlockSpec((DP, slots, 3 * hid), lambda i: (0, 0, 0)),
            pl.BlockSpec((EXPERTS, ROW, NB), lambda i: (0, 0, i)),
            pl.BlockSpec((EXPERTS * CAP, tokens.shape[0]), lambda i: (0, 0)),
        ],
        out_specs=(
            pl.BlockSpec((tokens.shape[0], 2 * NB), lambda i: (0, i)),
            pl.BlockSpec((columns, hid), lambda i: (i, 0)),
            pl.BlockSpec((columns, hid), lambda i: (i, 0)),
            pl.BlockSpec((hid, columns), lambda i: (0, i)),
        ),
        scratch_shapes=[pltpu.VMEM((hid, DP * slots), bf16)],
        compiler_params=pltpu.CompilerParams(vmem_limit_bytes=20 * 1024 * 1024),
        cost_estimate=pl.CostEstimate(
            flops=3 * 2 * slots * width * hid, bytes_accessed=18_000_000, transcendentals=0
        ),
    )(xbuf, dall, fin, pick)


def solution(mesh):
    in_specs = (
        P(("dp", "expert"), None),
        P(("dp", "expert"), None),
        P(("dp", "expert"), None),
        P(("dp", "expert"), None),
        P(None, "expert"),
        P(None, "expert"),
        P("expert", None),
    )
    out_specs = (P(("dp", "expert"), None), P("dp", "expert"), P("dp", "expert"), P("expert", "dp"))
    return jax.shard_map(body, mesh=mesh, in_specs=in_specs, out_specs=out_specs, check_vma=False)
```
